128 devices in a mesh: pop: 8 (over z, core), mp: 16 (over x, y).
Axes of the slice: x: 4, y: 4, z: 4, core: 2. Of those that a mesh axis runs over, the one named last changes fastest.
Arguments:
- weight: bfloat16 [4096, 16384], P(None, 'mp'), may hold values from -0.09375 to 0.09375
- layer_input: bfloat16 [16384, 4096], P('pop', 'mp'), may hold values from -17 to 17
- cotangent: bfloat16 [16384, 16384], P('pop', 'mp'), may hold values from -6 to 6
- factor_left: bfloat16 [128, 4096], replicated, may hold values from -6 to 6
- factor_right: bfloat16 [128, 16384], P(None, 'mp'), may hold values from -6 to 6
- seeds: int32 [128], P('pop'), may hold values from 0 to 127, each once
Outputs:
- estimate: float32 [4096, 16384], P('pop', 'mp')
- fitness: float32 [128], P('pop')
The draws below stay inside these ranges and needn't reach their ends.
Inputs may be any that keep to these rules, and one draw needn't show every extreme that they name: seeds is a permutation: each table row belongs to exactly one member.
All inputs are finite; a program needn't handle non-finite values.
Results may differ from the reference program's by a relative error of at most 0.0003.
Values may be sent and summed in bfloat16 or wider, within the bound.
No kernel may reach another device: no remote copies, remote signals or barrier semaphores. Data moves between devices by JAX's collectives and lax.ppermute only.
A program may use at most 128 MiB of HBM per device.

```python
import math
import jax
import jax.numpy as jnp
from jax import lax

D = 4096
FF = 16384
TOK = 128
MEMBERS = 128
ROWS = 16384


def draw_layer_input(key, part):
    key = jax.random.fold_in(key, 11)
    key_spread, key_body = jax.random.split(key, 2)
    member_index = jnp.arange(MEMBERS).astype(jnp.float32)
    spread = jax.random.uniform(key_spread, (MEMBERS,), minval=0.0, maxval=1.0)
    member_scale = 0.5 * jnp.exp(0.5 * jnp.log(10.0) * spread + 0.5 * jnp.log(3.0) * member_index / MEMBERS)
    row_scale = jnp.repeat(member_scale, TOK)
    values = jnp.clip(jax.random.normal(key_body, (ROWS, D)), -6.0, 6.0)
    return (values * row_scale[:, None]).astype(jnp.bfloat16)


def shard_levels(own_key, dims, pieces, smallest, high):
    loudness = 1.0
    for dim, parts in pieces:
        heights = jax.random.uniform(jax.random.fold_in(jax.random.fold_in(own_key, 6), dim), (parts,), jnp.float32, smallest / len(pieces), high / len(pieces))
        loudness = loudness * jnp.repeat(jnp.exp(heights), dims[dim] // parts).reshape((-1,) + (1,) * (len(dims) - 1 - dim))
    return loudness


def bell_draw(stream_key, shape, deviation, reach, shards=(), kind=jnp.bfloat16):
    level = shard_levels(stream_key, shape, shards, -0.22, 0.18) if shards else 1.0
    drawn = jax.random.normal(stream_key, shape, jnp.float32) * deviation * level
    return jnp.minimum(jnp.maximum(drawn, -reach), reach).astype(kind)


def setup_inputs(seed: int = 0) -> dict:
    keys = jax.random.split(jax.random.key(seed), 7)
    return {
        "weight": bell_draw(keys[0], (D, FF), D ** -0.5, 0.09375, ((1, 16),)),
        "layer_input": draw_layer_input(jax.random.fold_in(keys[6], 71), 0),
        "cotangent": bell_draw(keys[2], (ROWS, FF), 1.0, 6.0, ((0, 8), (1, 16))),
        "factor_left": bell_draw(keys[3], (MEMBERS, D), 1.0, 6.0),
        "factor_right": bell_draw(keys[4], (MEMBERS, FF), 1.0, 6.0, ((1, 16),)),
        "seeds": jax.random.permutation(keys[5], MEMBERS).astype(jnp.int32),
    }


perturb_scale = 0.25
epsilon = 1e-05

def reference(weight, layer_input, cotangent, factor_left, factor_right, seeds):
    left_rows = factor_left[seeds]
    right_rows = factor_right[seeds]
    grouped_input = layer_input.reshape(MEMBERS, TOK, D)
    grouped_cot = cotangent.reshape(MEMBERS, TOK, FF)

    def score_member(member_items):
        member_rows, member_cot, left_vec, right_vec = member_items
        base_sum = jnp.dot(member_rows, weight, preferred_element_type=jnp.float32)
        projected = jnp.dot(member_rows, left_vec, preferred_element_type=jnp.float32) * (perturb_scale / math.sqrt(D))
        preact = base_sum + projected[:, None] * right_vec.astype(jnp.float32)[None, :]
        squared = jnp.square(jax.nn.relu(preact))
        return -jnp.sum(member_cot.astype(jnp.float32) * squared) / math.sqrt(TOK * FF)
    fitness = lax.map(score_member, (grouped_input, grouped_cot, left_rows, right_rows))
    average = jnp.mean(fitness)
    variance = jnp.mean(jnp.square(fitness - average))
    shaped = (fitness - average) / jnp.sqrt(variance + epsilon)
    member_weights = shaped / math.sqrt(MEMBERS)
    scaled = left_rows.astype(jnp.float32) * member_weights[:, None]
    estimate = jnp.dot(scaled.T, right_rows.astype(jnp.float32), precision=lax.Precision.HIGHEST)
    return (estimate, fitness)
```

```python
import functools
import math

import jax
import jax.numpy as jnp
from jax import lax
from jax.experimental import pallas as pl
from jax.experimental.pallas import tpu as pltpu
from jax.sharding import PartitionSpec as P

D = 4096
FF = 16384
TOK = 128
SIDE = 4

perturb_scale = 0.25
epsilon = 1e-05

ROWS_PER_CHUNK = 512
COLS = 256
LANES = 128


def shift(piece, dx, dy):
    perm = [
        (x * SIDE + y, ((x + dx) % SIDE) * SIDE + (y + dy) % SIDE)
        for x in range(SIDE)
        for y in range(SIDE)
    ]
    return lax.ppermute(piece, "mp", perm)


def gather_chunk(piece, x_first):
    step = (lambda a, k: shift(a, k, 0)) if x_first else (lambda a, k: shift(a, 0, k))
    leap = (lambda a, k: shift(a, 0, k)) if x_first else (lambda a, k: shift(a, k, 0))
    block = jnp.concatenate([piece] + [step(piece, k) for k in range(1, SIDE)], axis=1)
    return [block] + [leap(block, k) for k in range(1, SIDE)]


def score_kernel(members, x0, x1, x2, x3, w_ref, left_ref, right_ref, cot_ref, pick_ref, out_ref, proj_ref):
    blocks = (x0, x1, x2, x3)
    col = pl.program_id(0)

    @pl.when(col == 0)
    def _():
        total = jnp.zeros(proj_ref.shape, jnp.float32)
        for j in range(SIDE):
            total += jnp.dot(blocks[j][...], left_ref[j], preferred_element_type=jnp.float32)
        proj_ref[...] = jnp.sum(
            jnp.where(pick_ref[...] > 0, total, 0.0), axis=1, keepdims=True
        ) * (perturb_scale / math.sqrt(D)) + jnp.zeros(proj_ref.shape, jnp.float32)
        out_ref[...] = jnp.zeros(out_ref.shape, jnp.float32)

    base = jnp.dot(x0[...], w_ref[0], preferred_element_type=jnp.float32)
    for j in range(1, SIDE):
        base += jnp.dot(blocks[j][...], w_ref[j], preferred_element_type=jnp.float32)
    for m in range(members):
        rows = slice(m * TOK, (m + 1) * TOK)
        proj = proj_ref[rows, :]
        right = right_ref[m : m + 1, :].astype(jnp.float32)
        for g in range(COLS // LANES):
            cols = slice(g * LANES, (g + 1) * LANES)
            act = jnp.maximum(base[rows, cols] + proj * right[:, cols], 0.0)
            term = cot_ref[rows, cols].astype(jnp.float32) * (act * act)
            out_ref[m : m + 1, :] += jnp.sum(term, axis=0, keepdims=True)


def score_chunk(blocks, w_perm, left_perm, right_rows, cot, pick, chunk):
    rows, extent = blocks[0].shape
    width = w_perm.shape[2]
    members = rows // TOK
    return pl.pallas_call(
        functools.partial(score_kernel, members),
        grid=(width // COLS,),
        in_specs=[pl.BlockSpec((rows, extent), lambda n: (0, 0))] * SIDE
        + [
            pl.BlockSpec((SIDE, extent, COLS), lambda n: (0, 0, n)),
            pl.BlockSpec((SIDE, extent, LANES), lambda n: (0, 0, 0)),
            pl.BlockSpec((members, COLS), lambda n: (0, n)),
            pl.BlockSpec((rows, COLS), lambda n: (chunk, n)),
            pl.BlockSpec((rows, LANES), lambda n: (0, 0)),
        ],
        out_specs=pl.BlockSpec((members, LANES), lambda n: (0, 0)),
        out_shape=jax.ShapeDtypeStruct((members, LANES), jnp.float32),
        scratch_shapes=[pltpu.VMEM((rows, LANES), jnp.float32)],
        compiler_params=pltpu.CompilerParams(vmem_limit_bytes=48 * 1024 * 1024),
        cost_estimate=pl.CostEstimate(
            flops=2 * rows * SIDE * extent * width,
            bytes_accessed=2 * SIDE * extent * (rows + width) + 2 * rows * width,
            transcendentals=0,
        ),
    )(*blocks, w_perm, left_perm, right_rows, cot, pick)


def reorder(array, x_first):
    here = lax.axis_index("mp")
    x, y = here // SIDE, here % SIDE
    width = array.shape[0] // (SIDE * SIDE)
    groups = []
    for j in range(SIDE):
        parts = []
        for i in range(SIDE):
            dx, dy = (i, j) if x_first else (j, i)
            source = lax.rem(x + SIDE - dx, SIDE) * SIDE + lax.rem(y + SIDE - dy, SIDE)
            parts.append(lax.dynamic_slice_in_dim(array, source * width, width, 0))
        groups.append(jnp.concatenate(parts, axis=0))
    return jnp.stack(groups)


def per_device(weight, layer_input, cotangent, factor_left, factor_right, seeds):
    members = factor_left.shape[0]
    owned = seeds.shape[0]
    rows = layer_input.shape[0]
    chunks = rows // ROWS_PER_CHUNK
    group = ROWS_PER_CHUNK // TOK

    orders = [c % 2 == 0 for c in range(chunks)]
    gathered = [
        gather_chunk(layer_input[c * ROWS_PER_CHUNK : (c + 1) * ROWS_PER_CHUNK], orders[c])
        for c in range(chunks)
    ]

    placement = (seeds[:, None] == jnp.arange(members, dtype=jnp.int32)[None, :]).astype(jnp.float32)
    picked = placement.astype(jnp.bfloat16)
    left_own = jnp.dot(factor_left.T, picked.T, preferred_element_type=jnp.float32).astype(jnp.bfloat16)
    left_own = jnp.pad(left_own, ((0, 0), (0, LANES - owned)))
    right_own = jnp.dot(picked, factor_right, preferred_element_type=jnp.float32).astype(jnp.bfloat16)
    w_perm = {o: reorder(weight, o) for o in (True, False)}
    left_perm = {o: reorder(left_own, o) for o in (True, False)}

    sums = []
    for c in range(chunks):
        member = c * group + jnp.arange(ROWS_PER_CHUNK, dtype=jnp.int32) // TOK
        pick = (member[:, None] == jnp.arange(LANES, dtype=jnp.int32)[None, :]).astype(jnp.float32)
        sums.append(
            score_chunk(
                gathered[c],
                w_perm[orders[c]],
                left_perm[orders[c]],
                right_own[c * group : (c + 1) * group],
                cotangent,
                pick,
                c,
            )
        )
    partial = -jnp.sum(jnp.concatenate(sums, axis=0), axis=1) / math.sqrt(TOK * FF)
    table = jnp.sum(placement * partial[:, None], 0)

    everywhere = ("pop", "mp")
    devices = lax.axis_size("pop") * lax.axis_size("mp")
    copies = jnp.broadcast_to(table[None, :], (devices, members))
    fitness_table = jnp.sum(lax.all_to_all(copies, everywhere, 0, 0, tiled=True), 0)
    fitness_own = jnp.sum(placement * fitness_table[None, :], 1)

    average = jnp.mean(fitness_table)
    variance = jnp.mean(jnp.square(fitness_table - average))
    shaped = (fitness_table - average) / jnp.sqrt(variance + epsilon)
    weights_table = shaped / math.sqrt(members)
    row_share = weight.shape[0] // lax.axis_size("pop")
    offset = lax.axis_index("pop") * row_share
    left_block = (
        lax.dynamic_slice_in_dim(factor_left, offset, row_share, 1).astype(jnp.float32)
        * weights_table[:, None]
    )
    estimate = jnp.dot(
        left_block.T, factor_right.astype(jnp.float32), precision=lax.Precision.HIGHEST
    )
    return (estimate, fitness_own)


def solution(mesh):
    placed = (P(None, "mp"), P("pop", "mp"), P("pop", "mp"), P(), P(None, "mp"), P("pop"))
    return jax.shard_map(
        per_device,
        mesh=mesh,
        in_specs=placed,
        out_specs=(P("pop", "mp"), P("pop")),
        check_vma=False,
    )
```

```python
import functools
import math

import jax
import jax.numpy as jnp
from jax import lax
from jax.experimental import pallas as pl
from jax.experimental.pallas import tpu as pltpu
from jax.sharding import PartitionSpec as P

D = 4096
FF = 16384
TOK = 128
SIDE = 4
STEPS = (0, 1, -1, 2)

perturb_scale = 0.25
epsilon = 1e-05

COLS = 256
LANES = 128


def shift(piece, dx, dy):
    perm = [
        (x * SIDE + y, ((x + dx) % SIDE) * SIDE + (y + dy) % SIDE)
        for x in range(SIDE)
        for y in range(SIDE)
    ]
    return lax.ppermute(piece, "mp", perm)


def one_ring(piece, along_x):
    step = (lambda a, k: shift(a, k, 0)) if along_x else (lambda a, k: shift(a, 0, k))
    half = piece.shape[0] // 2
    back, ahead = step(piece, 1), step(piece, -1)
    return back, ahead, step(back[:half], 1), step(ahead[half:], -1)


def near_kernel(idx_ref, b0, b1, b2, left_ref, *rest):
    w_refs, (out_ref, proj_ref) = rest[:-2], rest[-2:]
    blocks = (b0, b1, b2)

    @pl.when(pl.program_id(0) == 0)
    def _():
        total = jnp.dot(b0[...], left_ref[0], preferred_element_type=jnp.float32)
        for j in (1, 2):
            total += jnp.dot(blocks[j][...], left_ref[j], preferred_element_type=jnp.float32)
        proj_ref[...] = total

    total = None
    for j in range(3):
        w = jnp.concatenate([r[...] for r in w_refs[j * SIDE : (j + 1) * SIDE]], axis=0)
        part = jnp.dot(blocks[j][...], w, preferred_element_type=jnp.float32)
        total = part if total is None else total + part
    out_ref[...] = total


def w_specs(count, first, width):
    return [
        pl.BlockSpec((width, COLS), functools.partial(lambda k, n, idx: (idx[k], n), first + k))
        for k in range(count)
    ]


def near(blocks, idx, left_perm, weight):
    rows, extent = blocks[0].shape
    columns = weight.shape[1]
    whole = lambda n, idx: (0, 0)
    return pl.pallas_call(
        near_kernel,
        grid_spec=pltpu.PrefetchScalarGridSpec(
            num_scalar_prefetch=1,
            grid=(columns // COLS,),
            in_specs=[pl.BlockSpec((rows, extent), whole)] * 3
            + [pl.BlockSpec((3, extent, LANES), lambda n, idx: (0, 0, 0))]
            + w_specs(3 * SIDE, 0, extent // SIDE),
            out_specs=[
                pl.BlockSpec((rows, COLS), lambda n, idx: (0, n)),
                pl.BlockSpec((rows, LANES), whole),
            ],
        ),
        out_shape=[
            jax.ShapeDtypeStruct((rows, columns), jnp.float32),
            jax.ShapeDtypeStruct((rows, LANES), jnp.float32),
        ],
        compiler_params=pltpu.CompilerParams(vmem_limit_bytes=48 * 1024 * 1024),
        cost_estimate=pl.CostEstimate(
            flops=6 * rows * extent * columns,
            bytes_accessed=6 * extent * (rows + columns) + 4 * rows * columns,
            transcendentals=0,
        ),
    )(idx, *blocks, left_perm[:3], *([weight] * (3 * SIDE)))


def far_kernel(first, idx_ref, x_ref, left_ref, near_ref, near_proj_ref, right_ref, cot_ref, *rest):
    w_refs, (out_ref, proj_ref) = rest[:-2], rest[-2:]
    rows = x_ref.shape[0]

    @pl.when(pl.program_id(0) == 0)
    def _():
        total = near_proj_ref[...] + jnp.dot(
            x_ref[...], left_ref[0], preferred_element_type=jnp.float32
        )
        for m in range(rows // TOK):
            span = slice(m * TOK, (m + 1) * TOK)
            proj_ref[span, :] = jnp.broadcast_to(
                total[span, first + m : first + m + 1] * (perturb_scale / math.sqrt(D)),
                (TOK, LANES),
            )
        out_ref[...] = jnp.zeros(out_ref.shape, jnp.float32)

    w = jnp.concatenate([r[...] for r in w_refs], axis=0)
    base = near_ref[...] + jnp.dot(x_ref[...], w, preferred_element_type=jnp.float32)
    for m in range(rows // TOK):
        span = slice(m * TOK, (m + 1) * TOK)
        proj = proj_ref[span, :]
        right = right_ref[first + m : first + m + 1, :]
        sums = jnp.zeros((1, LANES), jnp.float32)
        for g in range(COLS // LANES):
            cols = slice(g * LANES, (g + 1) * LANES)
            act = jnp.maximum(base[span, cols] + proj * right[:, cols], 0.0)
            term = cot_ref[span, cols].astype(jnp.float32) * (act * act)
            sums += jnp.sum(term, axis=0, keepdims=True)
        out_ref[m : m + 1, :] += sums


def far(x, near_row, row, idx, left_perm, weight, near_sum, near_proj, right_own, cot):
    rows, extent = x.shape
    columns = weight.shape[1]
    members = rows // TOK
    whole = lambda n, idx: (0, 0)
    return pl.pallas_call(
        functools.partial(far_kernel, row // TOK),
        grid_spec=pltpu.PrefetchScalarGridSpec(
            num_scalar_prefetch=1,
            grid=(columns // COLS,),
            in_specs=[
                pl.BlockSpec((rows, extent), whole),
                pl.BlockSpec((1, extent, LANES), lambda n, idx: (3, 0, 0)),
                pl.BlockSpec((rows, COLS), lambda n, idx: (near_row // rows, n)),
                pl.BlockSpec((rows, LANES), lambda n, idx: (near_row // rows, 0)),
                pl.BlockSpec((right_own.shape[0], COLS), lambda n, idx: (0, n)),
                pl.BlockSpec((rows, COLS), lambda n, idx: (row // rows, n)),
            ]
            + w_specs(SIDE, 3 * SIDE, extent // SIDE),
            out_specs=pl.BlockSpec((members, LANES), whole),
            scratch_shapes=[pltpu.VMEM((rows, LANES), jnp.float32)],
        ),
        out_shape=jax.ShapeDtypeStruct((members, LANES), jnp.float32),
        compiler_params=pltpu.CompilerParams(vmem_limit_bytes=48 * 1024 * 1024),
        cost_estimate=pl.CostEstimate(
            flops=2 * rows * extent * columns,
            bytes_accessed=2 * extent * (rows + columns) + 6 * rows * columns,
            transcendentals=0,
        ),
    )(idx, x, left_perm, near_sum, near_proj, right_own, cot, *([weight] * SIDE))


def sources(x_first):
    here = lax.axis_index("mp")
    x, y = here // SIDE, here % SIDE
    steps = jnp.array(STEPS, dtype=jnp.int32)
    if x_first:
        index = ((x - steps[None, :]) % SIDE) * SIDE + (y - steps[:, None]) % SIDE
    else:
        index = ((x - steps[:, None]) % SIDE) * SIDE + (y - steps[None, :]) % SIDE
    return index.reshape(-1).astype(jnp.int32)


def per_device(weight, layer_input, cotangent, factor_left, factor_right, seeds):
    members = factor_left.shape[0]
    owned = seeds.shape[0]
    rows = layer_input.shape[0]
    half = rows // 2
    quarter = rows // 4

    pieces = {True: layer_input[:half], False: layer_input[half:]}
    rings = {}
    for o in (True, False):
        back, ahead, far0, far1 = one_ring(pieces[o], o)
        block = jnp.concatenate(
            [pieces[o], back, ahead, jnp.concatenate([far0, far1], axis=0)], axis=1
        )
        rings[o] = (block,) + one_ring(block, not o)

    placement = (seeds[:, None] == jnp.arange(members, dtype=jnp.int32)[None, :]).astype(jnp.float32)
    picked = placement.astype(jnp.bfloat16)
    left_own = jnp.dot(factor_left.T, picked.T, preferred_element_type=jnp.float32).astype(jnp.bfloat16)
    left_own = jnp.pad(left_own, ((0, 0), (0, LANES - owned)))
    right_own = jnp.dot(picked, factor_right, preferred_element_type=jnp.float32)
    width = layer_input.shape[1]

    sums = []
    for o in (True, False):
        idx = sources(o)
        left_perm = jnp.take(left_own.reshape(-1, width, LANES), idx, axis=0).reshape(
            SIDE, SIDE * width, LANES
        )
        block, back, ahead, far0, far1 = rings[o]
        near_sum, near_proj = near((block, back, ahead), idx, left_perm, weight)
        for k, piece in enumerate((far0, far1)):
            row = (0 if o else half) + k * quarter
            sums.append(
                far(
                    piece, k * quarter, row, idx, left_perm, weight,
                    near_sum, near_proj, right_own, cotangent,
                )
            )
    partial = -jnp.sum(jnp.concatenate(sums, axis=0), axis=1) / math.sqrt(TOK * FF)
    table = jnp.sum(placement * partial[:, None], 0)

    everywhere = ("pop", "mp")
    devices = lax.axis_size("pop") * lax.axis_size("mp")
    copies = jnp.broadcast_to(table[None, :], (devices, members))
    fitness_table = jnp.sum(lax.all_to_all(copies, everywhere, 0, 0, tiled=True), 0)
    fitness_own = jnp.sum(placement * fitness_table[None, :], 1)

    average = jnp.mean(fitness_table)
    variance = jnp.mean(jnp.square(fitness_table - average))
    shaped = (fitness_table - average) / jnp.sqrt(variance + epsilon)
    weights_table = shaped / math.sqrt(members)
    row_share = weight.shape[0] // lax.axis_size("pop")
    offset = lax.axis_index("pop") * row_share
    left_block = (
        lax.dynamic_slice_in_dim(factor_left, offset, row_share, 1).astype(jnp.float32)
        * weights_table[:, None]
    )
    estimate = jnp.dot(
        left_block.T, factor_right.astype(jnp.float32), precision=lax.Precision.HIGHEST
    )
    return (estimate, fitness_own)


def solution(mesh):
    placed = (P(None, "mp"), P("pop", "mp"), P("pop", "mp"), P(), P(None, "mp"), P("pop"))
    return jax.shard_map(
        per_device,
        mesh=mesh,
        in_specs=placed,
        out_specs=(P("pop", "mp"), P("pop")),
        check_vma=False,
    )
```

```python
import functools
import math

import jax
import jax.numpy as jnp
from jax import lax
from jax.experimental import pallas as pl
from jax.experimental.pallas import tpu as pltpu
from jax.sharding import PartitionSpec as P

D = 4096
FF = 16384
TOK = 128
SIDE = 4
STEPS = (0, 1, -1, 2)

perturb_scale = 0.25
epsilon = 1e-05

COLS = 256
LANES = 128
VMEM_LIMIT = 56 * 1024 * 1024


def shift(piece, dx, dy):
    perm = [
        (x * SIDE + y, ((x + dx) % SIDE) * SIDE + (y + dy) % SIDE)
        for x in range(SIDE)
        for y in range(SIDE)
    ]
    return lax.ppermute(piece, "mp", perm)


def first_ring(piece, along_x):
    step = (lambda a, k: shift(a, k, 0)) if along_x else (lambda a, k: shift(a, 0, k))
    half = piece.shape[0] // 2
    back, ahead = step(piece, 1), step(piece, -1)
    return back, ahead, step(back[:half], 1), step(ahead[half:], -1)


def stage_kernel(started, final, first, idx_ref, *refs):
    refs = list(refs)
    xs = [refs.pop(0) for _ in range(2)]
    w_refs = [[refs.pop(0) for _ in range(SIDE)] for _ in range(2)]
    left_refs = [[refs.pop(0) for _ in range(SIDE)] for _ in range(2)]
    sum_ref, sum_proj_ref = (refs.pop(0), refs.pop(0)) if started else (None, None)
    right_ref, cot_ref = (refs.pop(0), refs.pop(0)) if final else (None, None)
    out_ref, proj_ref = refs
    rows = xs[0].shape[0]

    @pl.when(pl.program_id(0) == 0)
    def _():
        for h in range(2):
            span = slice(h * rows, (h + 1) * rows)
            left = jnp.concatenate([r[...] for r in left_refs[h]], axis=0)
            total = jnp.dot(xs[h][...], left, preferred_element_type=jnp.float32)
            if started:
                total += sum_proj_ref[span, :]
            if not final:
                proj_ref[span, :] = total
                continue
            for m in range(rows // TOK):
                token = slice(m * TOK, (m + 1) * TOK)
                slot = first + h * (rows // TOK) + m
                proj_ref[h * rows + m * TOK : h * rows + (m + 1) * TOK, :] = jnp.broadcast_to(
                    total[token, slot : slot + 1] * (perturb_scale / math.sqrt(D)), (TOK, LANES)
                )
        if final:
            out_ref[...] = jnp.zeros(out_ref.shape, jnp.float32)

    for h in range(2):
        span = slice(h * rows, (h + 1) * rows)
        w = jnp.concatenate([r[...] for r in w_refs[h]], axis=0)
        base = jnp.dot(xs[h][...], w, preferred_element_type=jnp.float32)
        if started:
            base += sum_ref[span, :]
        if not final:
            out_ref[span, :] = base
            continue
        for m in range(rows // TOK):
            token = slice(m * TOK, (m + 1) * TOK)
            there = slice(h * rows + m * TOK, h * rows + (m + 1) * TOK)
            slot = h * (rows // TOK) + m
            proj = proj_ref[there, :]
            right = right_ref[first + slot : first + slot + 1, :]
            sums = jnp.zeros((1, LANES), jnp.float32)
            for g in range(COLS // LANES):
                cols = slice(g * LANES, (g + 1) * LANES)
                act = jnp.maximum(base[token, cols] + proj * right[:, cols], 0.0)
                term = cot_ref[there, cols].astype(jnp.float32) * (act * act)
                sums += jnp.sum(term, axis=0, keepdims=True)
            out_ref[slot : slot + 1, :] += sums


def stage(pieces, groups, idx, weight, left_own, sums, score=None):
    rows, extent = pieces[0].shape
    columns = weight.shape[1]
    width = extent // SIDE
    whole = lambda n, idx: (0, 0)
    block = pl.BlockSpec((2 * rows, COLS), lambda n, idx: (0, n))
    lane = pl.BlockSpec((2 * rows, LANES), whole)
    in_specs = [pl.BlockSpec((rows, extent), whole)] * 2
    operands = list(pieces)
    for array, size, moves in ((weight, COLS, 1), (left_own, LANES, 0)):
        for group in groups:
            for k in range(SIDE):
                place = functools.partial(
                    lambda at, moves, n, idx: (idx[at], n * moves), group * SIDE + k, moves
                )
                in_specs.append(pl.BlockSpec((width, size), place))
                operands.append(array)
    if sums is not None:
        in_specs += [block, lane]
        operands += list(sums)
    first = 0
    if score is None:
        out_specs, scratch = [block, lane], []
        out_shape = [
            jax.ShapeDtypeStruct((2 * rows, columns), jnp.float32),
            jax.ShapeDtypeStruct((2 * rows, LANES), jnp.float32),
        ]
    else:
        right_own, cot, part = score
        members = 2 * rows // TOK
        first = part * members
        in_specs += [
            pl.BlockSpec((right_own.shape[0], COLS), lambda n, idx: (0, n)),
            pl.BlockSpec((2 * rows, COLS), lambda n, idx: (part, n)),
        ]
        operands += [right_own, cot]
        out_specs = pl.BlockSpec((members, LANES), whole)
        out_shape = jax.ShapeDtypeStruct((members, LANES), jnp.float32)
        scratch = [pltpu.VMEM((2 * rows, LANES), jnp.float32)]
    return pl.pallas_call(
        functools.partial(stage_kernel, sums is not None, score is not None, first),
        grid_spec=pltpu.PrefetchScalarGridSpec(
            num_scalar_prefetch=1,
            grid=(columns // COLS,),
            in_specs=in_specs,
            out_specs=out_specs,
            scratch_shapes=scratch,
        ),
        out_shape=out_shape,
        compiler_params=pltpu.CompilerParams(vmem_limit_bytes=VMEM_LIMIT),
        cost_estimate=pl.CostEstimate(
            flops=4 * rows * extent * columns,
            bytes_accessed=4 * extent * (rows + columns) + 16 * rows * columns,
            transcendentals=0,
        ),
    )(idx, *operands)


def finish_kernel(owned, at_ref, tables_ref, seat_ref, left_ref, right_ref, est_ref, fit_ref):
    members = tables_ref.shape[1]
    row = jnp.sum(tables_ref[...], axis=0, keepdims=True)
    shape = (members, members)
    same = lax.broadcasted_iota(jnp.int32, shape, 0) == lax.broadcasted_iota(jnp.int32, shape, 1)
    column = jnp.sum(
        jnp.where(same, jnp.broadcast_to(row, shape), 0.0), axis=1, keepdims=True
    )
    fit_ref[...] = jnp.sum(seat_ref[...] * column, axis=0, keepdims=True)[:, :owned]
    average = jnp.sum(row) / members
    variance = jnp.sum(jnp.square(row - average)) / members
    spread = jnp.sqrt(jnp.full((members, 1), variance + epsilon, jnp.float32))
    weights = (column - average) / spread / math.sqrt(members)
    scaled = left_ref[...].astype(jnp.float32) * weights
    high = scaled.astype(jnp.bfloat16)
    rest = scaled - high.astype(jnp.float32)
    middle = rest.astype(jnp.bfloat16)
    low = (rest - middle.astype(jnp.float32)).astype(jnp.bfloat16)
    total = None
    for term in (low, middle, high):
        part = lax.dot_general(
            term, right_ref[...], (((0,), (0,)), ((), ())), preferred_element_type=jnp.float32
        )
        total = part if total is None else total + part
    est_ref[...] = total


def finish(at, tables, seat, factor_left, factor_right, owned, row_share):
    devices, members = tables.shape
    columns = factor_right.shape[1]
    return pl.pallas_call(
        functools.partial(finish_kernel, owned),
        grid_spec=pltpu.PrefetchScalarGridSpec(
            num_scalar_prefetch=1,
            grid=(1,),
            in_specs=[
                pl.BlockSpec((devices, members), lambda n, at: (0, 0)),
                pl.BlockSpec((members, LANES), lambda n, at: (0, 0)),
                pl.BlockSpec((members, row_share), lambda n, at: (0, at[0])),
                pl.BlockSpec((members, columns), lambda n, at: (0, 0)),
            ],
            out_specs=[
                pl.BlockSpec((row_share, columns), lambda n, at: (0, 0)),
                pl.BlockSpec((1, owned), lambda n, at: (0, 0)),
            ],
        ),
        out_shape=[
            jax.ShapeDtypeStruct((row_share, columns), jnp.float32),
            jax.ShapeDtypeStruct((1, owned), jnp.float32),
        ],
        compiler_params=pltpu.CompilerParams(vmem_limit_bytes=VMEM_LIMIT),
    )(at, tables, seat, factor_left, factor_right)


def sources(x_first):
    here = lax.axis_index("mp")
    x, y = here // SIDE, here % SIDE
    steps = jnp.array(STEPS, dtype=jnp.int32)
    if x_first:
        index = ((x - steps[None, :]) % SIDE) * SIDE + (y - steps[:, None]) % SIDE
    else:
        index = ((x - steps[:, None]) % SIDE) * SIDE + (y - steps[None, :]) % SIDE
    return index.reshape(-1).astype(jnp.int32)


def per_device(weight, layer_input, cotangent, factor_left, factor_right, seeds):
    members = factor_left.shape[0]
    owned = seeds.shape[0]
    rows = layer_input.shape[0]
    half = rows // 2
    quarter = rows // 4

    pieces = {True: layer_input[:half], False: layer_input[half:]}
    blocks = {}
    for o in (True, False):
        back, ahead, far0, far1 = first_ring(pieces[o], o)
        blocks[o] = [
            jnp.concatenate([pieces[o][s], back[s], ahead[s], far], axis=1)
            for s, far in ((slice(0, quarter), far0), (slice(quarter, half), far1))
        ]

    slots = jnp.pad(seeds, (0, LANES - owned), constant_values=-1)
    seat = slots[None, :] == jnp.arange(members, dtype=jnp.int32)[:, None]
    picked = seat.astype(jnp.bfloat16)
    contract = (((0,), (0,)), ((), ()))
    left_own = lax.dot_general(
        factor_left, picked, contract, preferred_element_type=jnp.float32
    ).astype(jnp.bfloat16)
    right_own = lax.dot_general(
        picked[:, :owned], factor_right, contract, preferred_element_type=jnp.float32
    )

    both = (True, False)
    ways = (1, -1)
    idx = {o: sources(o) for o in both}
    score = {o: (right_own, cotangent, 0 if o else 1) for o in both}

    def send(arrays, o, sense):
        return [
            shift(a, 0, sense * way) if o else shift(a, sense * way, 0)
            for a, way in zip(arrays, ways)
        ]

    near = {o: send(blocks[o], o, 1) for o in both}
    sums = {o: stage(blocks[o], (0, 0), idx[o], weight, left_own, None) for o in both}
    near, sums = lax.optimization_barrier((near, sums))
    far = {o: send(near[o], o, 1) for o in both}
    sums = {o: stage(near[o], (1, 2), idx[o], weight, left_own, sums[o]) for o in both}
    far, sums, blocks = lax.optimization_barrier((far, sums, blocks))
    other = {o: send(blocks[o], o, -1) for o in both}
    sums = {o: stage(far[o], (3, 3), idx[o], weight, left_own, sums[o]) for o in both}
    scores = [
        stage(other[o], (2, 1), idx[o], weight, left_own, sums[o], score[o]) for o in both
    ]
    partial = -jnp.sum(jnp.concatenate(scores, axis=0), axis=1) / math.sqrt(TOK * FF)
    seated = seat[:, :owned].astype(jnp.float32)
    table = jnp.sum(seated * partial[None, :], 1)

    everywhere = ("pop", "mp")
    devices = lax.axis_size("pop") * lax.axis_size("mp")
    copies = jnp.broadcast_to(table[None, :], (devices, members))
    tables = lax.all_to_all(copies, everywhere, 0, 0, tiled=True)
    row_share = weight.shape[0] // lax.axis_size("pop")
    at = lax.axis_index("pop").astype(jnp.int32).reshape(1)
    estimate, fitness = finish(
        at, tables, seat.astype(jnp.float32), factor_left, factor_right, owned, row_share
    )
    return (estimate, fitness.reshape(owned))


def solution(mesh):
    placed = (P(None, "mp"), P("pop", "mp"), P("pop", "mp"), P(), P(None, "mp"), P("pop"))
    return jax.shard_map(
        per_device,
        mesh=mesh,
        in_specs=placed,
        out_specs=(P("pop", "mp"), P("pop")),
        check_vma=False,
    )
```

```python
import functools
import math

import jax
import jax.numpy as jnp
from jax import lax
from jax.experimental import pallas as pl
from jax.experimental.pallas import tpu as pltpu
from jax.sharding import PartitionSpec as P

D = 4096
FF = 16384
TOK = 128
SIDE = 4
STEPS = (0, 1, -1, 2)

perturb_scale = 0.25
epsilon = 1e-05

COLS = 256
LANES = 128
VMEM_LIMIT = 48 * 1024 * 1024


def shift(piece, dx, dy):
    perm = [
        (x * SIDE + y, ((x + dx) % SIDE) * SIDE + (y + dy) % SIDE)
        for x in range(SIDE)
        for y in range(SIDE)
    ]
    return lax.ppermute(piece, "mp", perm)


def first_ring(piece, along_x):
    step = (lambda a, k: shift(a, k, 0)) if along_x else (lambda a, k: shift(a, 0, k))
    half = piece.shape[0] // 2
    back, ahead = step(piece, 1), step(piece, -1)
    return back, ahead, step(back[:half], 1), step(ahead[half:], -1)


def stage_kernel(terms, started, final, idx_ref, *refs):
    refs = list(refs)
    xs = [[refs.pop(0) for _ in block] for block in terms]
    w_ref, left_ref = refs.pop(0), refs.pop(0)
    sum_ref, sum_proj_ref = (refs.pop(0), refs.pop(0)) if started else (None, None)
    right_ref, cot_ref = (refs.pop(0), refs.pop(0)) if final else (None, None)
    out_ref, proj_ref = refs
    rows, extent = xs[0][0].shape
    width = extent // SIDE
    members = rows // TOK

    def product(b, ref):
        total = None
        for x_ref, place in zip(xs[b], terms[b]):
            parts = [
                ref[pl.ds(pl.multiple_of(idx_ref[place + k] * width, width), width), :]
                for k in range(SIDE)
            ]
            part = jnp.dot(
                x_ref[...], jnp.concatenate(parts, axis=0), preferred_element_type=jnp.float32
            )
            total = part if total is None else total + part
        return total

    @pl.when(pl.program_id(0) == 0)
    def _():
        for b in range(len(terms)):
            total = product(b, left_ref)
            if started:
                total += sum_proj_ref[b * rows : (b + 1) * rows, :]
            if not final:
                proj_ref[b * rows : (b + 1) * rows, :] = total
                continue
            for m in range(members):
                slot = b * members + m
                one = total[m * TOK : (m + 1) * TOK, slot : slot + 1]
                proj_ref[slot * TOK : (slot + 1) * TOK, :] = jnp.broadcast_to(
                    one * (perturb_scale / math.sqrt(D)), (TOK, LANES)
                )
        if final:
            out_ref[...] = jnp.zeros(out_ref.shape, jnp.float32)

    for b in range(len(terms)):
        base = product(b, w_ref)
        if started:
            base += sum_ref[b * rows : (b + 1) * rows, :]
        if not final:
            out_ref[b * rows : (b + 1) * rows, :] = base
            continue
        for m in range(members):
            slot = b * members + m
            token = slice(m * TOK, (m + 1) * TOK)
            there = slice(slot * TOK, (slot + 1) * TOK)
            proj = proj_ref[there, :]
            right = right_ref[slot : slot + 1, :]
            sums = jnp.zeros((1, LANES), jnp.float32)
            for g in range(COLS // LANES):
                cols = slice(g * LANES, (g + 1) * LANES)
                act = jnp.maximum(base[token, cols] + proj * right[:, cols], 0.0)
                term = cot_ref[there, cols].astype(jnp.float32) * (act * act)
                sums += jnp.sum(term, axis=0, keepdims=True)
            out_ref[slot : slot + 1, :] += sums


def stage(blocks, idx, weight, left_own, sums=None, score=None):
    terms = tuple(tuple(place for _, place in block) for block in blocks)
    rows, extent = blocks[0][0][0].shape
    total = rows * len(blocks)
    depth, columns = weight.shape
    whole = lambda n, idx: (0, 0)
    tile = lambda n, idx: (0, n)
    once = pl.Buffered(1)
    operands = [piece for block in blocks for piece, _ in block]
    in_specs = [pl.BlockSpec((rows, extent), whole, pipeline_mode=once)] * len(operands)
    in_specs += [
        pl.BlockSpec((depth, COLS), tile),
        pl.BlockSpec((depth, LANES), whole, pipeline_mode=once),
    ]
    operands += [weight, left_own]
    block = pl.BlockSpec((total, COLS), tile)
    if sums is not None:
        in_specs += [block, pl.BlockSpec((total, LANES), whole, pipeline_mode=once)]
        operands += list(sums)
    if score is None:
        out_specs, scratch = [block, pl.BlockSpec((total, LANES), whole)], []
        out_shape = [
            jax.ShapeDtypeStruct((total, columns), jnp.float32),
            jax.ShapeDtypeStruct((total, LANES), jnp.float32),
        ]
    else:
        members = total // TOK
        in_specs += [pl.BlockSpec((members, COLS), tile), block]
        operands += list(score)
        out_specs = pl.BlockSpec((members, LANES), whole)
        out_shape = jax.ShapeDtypeStruct((members, LANES), jnp.float32)
        scratch = [pltpu.VMEM((total, LANES), jnp.float32)]
    flops = 2 * sum(len(t) for t in terms) * rows * extent * columns
    return pl.pallas_call(
        functools.partial(stage_kernel, terms, sums is not None, score is not None),
        grid_spec=pltpu.PrefetchScalarGridSpec(
            num_scalar_prefetch=1,
            grid=(columns // COLS,),
            in_specs=in_specs,
            out_specs=out_specs,
            scratch_shapes=scratch,
        ),
        out_shape=out_shape,
        compiler_params=pltpu.CompilerParams(vmem_limit_bytes=VMEM_LIMIT),
        cost_estimate=pl.CostEstimate(
            flops=flops, bytes_accessed=flops // 256, transcendentals=0
        ),
    )(idx, *operands)


def finish_kernel(owned, at_ref, tables_ref, seat_ref, left_ref, right_ref, est_ref, fit_ref):
    members = tables_ref.shape[1]
    row = jnp.sum(tables_ref[...], axis=0, keepdims=True)
    shape = (members, members)
    same = lax.broadcasted_iota(jnp.int32, shape, 0) == lax.broadcasted_iota(jnp.int32, shape, 1)
    column = jnp.sum(
        jnp.where(same, jnp.broadcast_to(row, shape), 0.0), axis=1, keepdims=True
    )
    fit_ref[...] = jnp.sum(seat_ref[...] * column, axis=0, keepdims=True)[:, :owned]
    average = jnp.sum(row) / members
    variance = jnp.sum(jnp.square(row - average)) / members
    spread = jnp.sqrt(jnp.full((members, 1), variance + epsilon, jnp.float32))
    weights = (column - average) / spread / math.sqrt(members)
    scaled = left_ref[...].astype(jnp.float32) * weights
    high = scaled.astype(jnp.bfloat16)
    rest = scaled - high.astype(jnp.float32)
    middle = rest.astype(jnp.bfloat16)
    low = (rest - middle.astype(jnp.float32)).astype(jnp.bfloat16)
    total = None
    for term in (low, middle, high):
        part = lax.dot_general(
            term, right_ref[...], (((0,), (0,)), ((), ())), preferred_element_type=jnp.float32
        )
        total = part if total is None else total + part
    est_ref[...] = total


def finish(at, tables, seat, factor_left, factor_right, owned, row_share):
    devices, members = tables.shape
    columns = factor_right.shape[1]
    return pl.pallas_call(
        functools.partial(finish_kernel, owned),
        grid_spec=pltpu.PrefetchScalarGridSpec(
            num_scalar_prefetch=1,
            grid=(1,),
            in_specs=[
                pl.BlockSpec((devices, members), lambda n, at: (0, 0)),
                pl.BlockSpec((members, LANES), lambda n, at: (0, 0)),
                pl.BlockSpec((members, row_share), lambda n, at: (0, at[0])),
                pl.BlockSpec((members, columns), lambda n, at: (0, 0)),
            ],
            out_specs=[
                pl.BlockSpec((row_share, columns), lambda n, at: (0, 0)),
                pl.BlockSpec((1, owned), lambda n, at: (0, 0)),
            ],
        ),
        out_shape=[
            jax.ShapeDtypeStruct((row_share, columns), jnp.float32),
            jax.ShapeDtypeStruct((1, owned), jnp.float32),
        ],
        compiler_params=pltpu.CompilerParams(vmem_limit_bytes=VMEM_LIMIT),
    )(at, tables, seat, factor_left, factor_right)


def sources(x_first):
    here = lax.axis_index("mp")
    x, y = here // SIDE, here % SIDE
    steps = jnp.array(STEPS, dtype=jnp.int32)
    if x_first:
        index = ((x - steps[None, :]) % SIDE) * SIDE + (y - steps[:, None]) % SIDE
    else:
        index = ((x - steps[:, None]) % SIDE) * SIDE + (y - steps[None, :]) % SIDE
    return index.reshape(-1).astype(jnp.int32)


def per_device(weight, layer_input, cotangent, factor_left, factor_right, seeds):
    members = factor_left.shape[0]
    owned = seeds.shape[0]
    rows = layer_input.shape[0]
    half = rows // 2
    quarter = rows // 4

    pieces = {True: layer_input[:half], False: layer_input[half:]}
    blocks = {}
    for o in (True, False):
        back, ahead, far0, far1 = first_ring(pieces[o], o)
        blocks[o] = [
            jnp.concatenate([pieces[o][s], back[s], ahead[s], far], axis=1)
            for s, far in ((slice(0, quarter), far0), (slice(quarter, half), far1))
        ]

    slots = jnp.pad(seeds, (0, LANES - owned), constant_values=-1)
    seat = slots[None, :] == jnp.arange(members, dtype=jnp.int32)[:, None]
    picked = seat.astype(jnp.bfloat16)
    contract = (((0,), (0,)), ((), ()))
    left_own = lax.dot_general(
        factor_left, picked, contract, preferred_element_type=jnp.float32
    ).astype(jnp.bfloat16)
    right_own = lax.dot_general(
        picked[:, :owned], factor_right, contract, preferred_element_type=jnp.float32
    )

    both = (True, False)
    ways = (1, -1)
    idx = jnp.concatenate([sources(o) for o in both])

    def send(arrays, o, sense):
        return [
            shift(a, 0, sense * way) if o else shift(a, sense * way, 0)
            for a, way in zip(arrays, ways)
        ]

    def terms(*given):
        out = []
        for base, o in ((0, True), (SIDE * SIDE, False)):
            for h in range(2):
                out.append([(arrays[o][h], base + SIDE * groups[h]) for arrays, groups in given])
        return out

    near = {o: send(blocks[o], o, 1) for o in both}
    far = {o: send(near[o], o, 1) for o in both}
    sums = stage(terms((blocks, (0, 0)), (near, (1, 2))), idx, weight, left_own)
    far, sums, blocks = lax.optimization_barrier((far, sums, blocks))
    other = {o: send(blocks[o], o, -1) for o in both}
    sums = stage(terms((far, (3, 3))), idx, weight, left_own, sums)
    scores = stage(
        terms((other, (2, 1))), idx, weight, left_own, sums, (right_own, cotangent)
    )
    partial = -jnp.sum(scores, axis=1) / math.sqrt(TOK * FF)
    seated = seat[:, :owned].astype(jnp.float32)
    table = jnp.sum(seated * partial[None, :], 1)

    everywhere = ("pop", "mp")
    devices = lax.axis_size("pop") * lax.axis_size("mp")
    copies = jnp.broadcast_to(table[None, :], (devices, members))
    tables = lax.all_to_all(copies, everywhere, 0, 0, tiled=True)
    row_share = weight.shape[0] // lax.axis_size("pop")
    at = lax.axis_index("pop").astype(jnp.int32).reshape(1)
    estimate, fitness = finish(
        at, tables, seat.astype(jnp.float32), factor_left, factor_right, owned, row_share
    )
    return (estimate, fitness.reshape(owned))


def solution(mesh):
    placed = (P(None, "mp"), P("pop", "mp"), P("pop", "mp"), P(), P(None, "mp"), P("pop"))
    return jax.shard_map(
        per_device,
        mesh=mesh,
        in_specs=placed,
        out_specs=(P("pop", "mp"), P("pop")),
        check_vma=False,
    )
```

```python
import functools
import math

import jax
import jax.numpy as jnp
from jax import lax
from jax.experimental import pallas as pl
from jax.experimental.pallas import tpu as pltpu
from jax.sharding import PartitionSpec as P

D = 4096
FF = 16384
TOK = 128
SIDE = 4
STEPS = (0, 1, -1, 2)

perturb_scale = 0.25
epsilon = 1e-05

COLS = 256
LANES = 128
VMEM_LIMITS = (36 << 20, 26 << 20, 20 << 20)


def shift(piece, dx, dy):
    perm = [
        (x * SIDE + y, ((x + dx) % SIDE) * SIDE + (y + dy) % SIDE)
        for x in range(SIDE)
        for y in range(SIDE)
    ]
    return lax.ppermute(piece, "mp", perm)


def first_ring(piece, along_x):
    step = (lambda a, k: shift(a, k, 0)) if along_x else (lambda a, k: shift(a, 0, k))
    half = piece.shape[0] // 2
    back, ahead = step(piece, 1), step(piece, -1)
    return back, ahead, step(back[:half], 1), step(ahead[half:], -1)


def stage_kernel(terms, started, final, idx_ref, *refs):
    refs = list(refs)
    xs = [[refs.pop(0) for _ in block] for block in terms]
    w_ref = None if final else refs.pop(0)
    w_refs = {t[0]: [refs.pop(0) for _ in range(SIDE)] for t in dict.fromkeys(terms)} if final else {}
    left_ref = refs.pop(0)
    sum_ref, sum_proj_ref = (refs.pop(0), refs.pop(0)) if started else (None, None)
    right_ref, cot_ref = (refs.pop(0), refs.pop(0)) if final else (None, None)
    out_ref, proj_ref = refs
    rows, extent = xs[0][0].shape
    width = extent // SIDE
    members = rows // TOK

    def product(b, ref):
        total = None
        for x_ref, place in zip(xs[b], terms[b]):
            if ref is None:
                parts = [part[...] for part in w_refs[place]]
            else:
                parts = [
                    ref[pl.ds(pl.multiple_of(idx_ref[place + k] * width, width), width), :]
                    for k in range(SIDE)
                ]
            part = jnp.dot(
                x_ref[...], jnp.concatenate(parts, axis=0), preferred_element_type=jnp.float32
            )
            total = part if total is None else total + part
        return total

    @pl.when(pl.program_id(0) == 0)
    def _():
        for b in range(len(terms)):
            total = product(b, left_ref)
            if started:
                total += sum_proj_ref[b * rows : (b + 1) * rows, :]
            if not final:
                proj_ref[b * rows : (b + 1) * rows, :] = total
                continue
            for m in range(members):
                slot = b * members + m
                one = total[m * TOK : (m + 1) * TOK, slot : slot + 1]
                proj_ref[slot * TOK : (slot + 1) * TOK, :] = jnp.broadcast_to(
                    one * (perturb_scale / math.sqrt(D)), (TOK, LANES)
                )
        if final:
            out_ref[...] = jnp.zeros(out_ref.shape, jnp.float32)

    for b in range(len(terms)):
        base = product(b, w_ref)
        if started:
            base += sum_ref[b * rows : (b + 1) * rows, :]
        if not final:
            out_ref[b * rows : (b + 1) * rows, :] = base
            continue
        for m in range(members):
            slot = b * members + m
            token = slice(m * TOK, (m + 1) * TOK)
            there = slice(slot * TOK, (slot + 1) * TOK)
            proj = proj_ref[there, :]
            right = right_ref[slot : slot + 1, :]
            sums = jnp.zeros((1, LANES), jnp.float32)
            for g in range(COLS // LANES):
                cols = slice(g * LANES, (g + 1) * LANES)
                act = jnp.maximum(base[token, cols] + proj * right[:, cols], 0.0)
                term = cot_ref[there, cols].astype(jnp.float32) * (act * act)
                sums += jnp.sum(term, axis=0, keepdims=True)
            out_ref[slot : slot + 1, :] += sums


def stage(blocks, idx, weight, left_own, limit, sums=None, score=None):
    terms = tuple(tuple(place for _, place in block) for block in blocks)
    rows, extent = blocks[0][0][0].shape
    total = rows * len(blocks)
    depth, columns = weight.shape
    whole = lambda n, idx: (0, 0)
    tile = lambda n, idx: (0, n)
    once = pl.Buffered(1)
    operands = [piece for block in blocks for piece, _ in block]
    in_specs = [pl.BlockSpec((rows, extent), whole, pipeline_mode=once)] * len(operands)
    if score is None:
        in_specs.append(pl.BlockSpec((depth, COLS), tile))
        operands.append(weight)
    else:
        for (place,) in dict.fromkeys(terms):
            for k in range(SIDE):
                row = functools.partial(lambda at, n, idx: (idx[at], n), place + k)
                in_specs.append(pl.BlockSpec((extent // SIDE, COLS), row))
                operands.append(weight)
    in_specs.append(pl.BlockSpec((depth, LANES), whole, pipeline_mode=once))
    operands.append(left_own)
    block = pl.BlockSpec((total, COLS), tile)
    if sums is not None:
        in_specs += [block, pl.BlockSpec((total, LANES), whole, pipeline_mode=once)]
        operands += list(sums)
    if score is None:
        out_specs, scratch = [block, pl.BlockSpec((total, LANES), whole)], []
        out_shape = [
            jax.ShapeDtypeStruct((total, columns), jnp.float32),
            jax.ShapeDtypeStruct((total, LANES), jnp.float32),
        ]
    else:
        members = total // TOK
        in_specs += [pl.BlockSpec((members, COLS), tile), block]
        operands += list(score)
        out_specs = pl.BlockSpec((members, LANES), whole)
        out_shape = jax.ShapeDtypeStruct((members, LANES), jnp.float32)
        scratch = [pltpu.VMEM((total, LANES), jnp.float32)]
    flops = 2 * sum(len(t) for t in terms) * rows * extent * columns
    return pl.pallas_call(
        functools.partial(stage_kernel, terms, sums is not None, score is not None),
        grid_spec=pltpu.PrefetchScalarGridSpec(
            num_scalar_prefetch=1,
            grid=(columns // COLS,),
            in_specs=in_specs,
            out_specs=out_specs,
            scratch_shapes=scratch,
        ),
        out_shape=out_shape,
        compiler_params=pltpu.CompilerParams(vmem_limit_bytes=limit),
        cost_estimate=pl.CostEstimate(
            flops=flops, bytes_accessed=flops // 256, transcendentals=0
        ),
    )(idx, *operands)


def finish_kernel(owned, at_ref, tables_ref, seat_ref, left_ref, right_ref, est_ref, fit_ref):
    members = tables_ref.shape[1]
    row = jnp.sum(tables_ref[...], axis=0, keepdims=True)
    shape = (members, members)
    same = lax.broadcasted_iota(jnp.int32, shape, 0) == lax.broadcasted_iota(jnp.int32, shape, 1)
    column = jnp.sum(
        jnp.where(same, jnp.broadcast_to(row, shape), 0.0), axis=1, keepdims=True
    )
    fit_ref[...] = jnp.sum(seat_ref[...] * column, axis=0, keepdims=True)[:, :owned]
    average = jnp.sum(row) / members
    variance = jnp.sum(jnp.square(row - average)) / members
    spread = jnp.sqrt(jnp.full((members, 1), variance + epsilon, jnp.float32))
    weights = (column - average) / spread / math.sqrt(members)
    scaled = left_ref[...].astype(jnp.float32) * weights
    high = scaled.astype(jnp.bfloat16)
    rest = scaled - high.astype(jnp.float32)
    middle = rest.astype(jnp.bfloat16)
    low = (rest - middle.astype(jnp.float32)).astype(jnp.bfloat16)
    total = None
    for term in (low, middle, high):
        part = lax.dot_general(
            term, right_ref[...], (((0,), (0,)), ((), ())), preferred_element_type=jnp.float32
        )
        total = part if total is None else total + part
    est_ref[...] = total


def finish(at, tables, seat, factor_left, factor_right, owned, row_share):
    devices, members = tables.shape
    columns = factor_right.shape[1]
    return pl.pallas_call(
        functools.partial(finish_kernel, owned),
        grid_spec=pltpu.PrefetchScalarGridSpec(
            num_scalar_prefetch=1,
            grid=(1,),
            in_specs=[
                pl.BlockSpec((devices, members), lambda n, at: (0, 0)),
                pl.BlockSpec((members, LANES), lambda n, at: (0, 0)),
                pl.BlockSpec((members, row_share), lambda n, at: (0, at[0])),
                pl.BlockSpec((members, columns), lambda n, at: (0, 0)),
            ],
            out_specs=[
                pl.BlockSpec((row_share, columns), lambda n, at: (0, 0)),
                pl.BlockSpec((1, owned), lambda n, at: (0, 0)),
            ],
        ),
        out_shape=[
            jax.ShapeDtypeStruct((row_share, columns), jnp.float32),
            jax.ShapeDtypeStruct((1, owned), jnp.float32),
        ],
        compiler_params=pltpu.CompilerParams(vmem_limit_bytes=VMEM_LIMITS[2]),
    )(at, tables, seat, factor_left, factor_right)


def sources(x_first):
    here = lax.axis_index("mp")
    x, y = here // SIDE, here % SIDE
    steps = jnp.array(STEPS, dtype=jnp.int32)
    if x_first:
        index = ((x - steps[None, :]) % SIDE) * SIDE + (y - steps[:, None]) % SIDE
    else:
        index = ((x - steps[:, None]) % SIDE) * SIDE + (y - steps[None, :]) % SIDE
    return index.reshape(-1).astype(jnp.int32)


def per_device(weight, layer_input, cotangent, factor_left, factor_right, seeds):
    members = factor_left.shape[0]
    owned = seeds.shape[0]
    rows = layer_input.shape[0]
    half = rows // 2
    quarter = rows // 4

    pieces = {True: layer_input[:half], False: layer_input[half:]}
    blocks = {}
    for o in (True, False):
        back, ahead, far0, far1 = first_ring(pieces[o], o)
        blocks[o] = [
            jnp.concatenate([pieces[o][s], back[s], ahead[s], far], axis=1)
            for s, far in ((slice(0, quarter), far0), (slice(quarter, half), far1))
        ]

    slots = jnp.pad(seeds, (0, LANES - owned), constant_values=-1)
    seat = slots[None, :] == jnp.arange(members, dtype=jnp.int32)[:, None]
    picked = seat.astype(jnp.bfloat16)
    contract = (((0,), (0,)), ((), ()))
    left_own = lax.dot_general(
        factor_left, picked, contract, preferred_element_type=jnp.float32
    ).astype(jnp.bfloat16)
    right_own = lax.dot_general(
        picked[:, :owned], factor_right, contract, preferred_element_type=jnp.float32
    )

    both = (True, False)
    ways = (1, -1)
    idx = jnp.concatenate([sources(o) for o in both])

    def send(arrays, o, sense):
        return [
            shift(a, 0, sense * way) if o else shift(a, sense * way, 0)
            for a, way in zip(arrays, ways)
        ]

    def terms(*given):
        out = []
        for base, o in ((0, True), (SIDE * SIDE, False)):
            for h in range(2):
                out.append([(arrays[o][h], base + SIDE * groups[h]) for arrays, groups in given])
        return out

    near = {o: send(blocks[o], o, 1) for o in both}
    near, blocks = lax.optimization_barrier((near, blocks))
    other = {o: send(blocks[o], o, -1) for o in both}
    sums = stage(terms((blocks, (0, 0)), (near, (1, 2))), idx, weight, left_own, VMEM_LIMITS[0])
    other, sums, near = lax.optimization_barrier((other, sums, near))
    far = {o: send(near[o], o, 1) for o in both}
    sums = stage(terms((other, (2, 1))), idx, weight, left_own, VMEM_LIMITS[1], sums)
    scores = stage(
        terms((far, (3, 3))), idx, weight, left_own, VMEM_LIMITS[2], sums, (right_own, cotangent)
    )
    partial = -jnp.sum(scores, axis=1) / math.sqrt(TOK * FF)
    seated = seat[:, :owned].astype(jnp.float32)
    table = jnp.sum(seated * partial[None, :], 1)

    everywhere = ("pop", "mp")
    devices = lax.axis_size("pop") * lax.axis_size("mp")
    copies = jnp.broadcast_to(table[None, :], (devices, members))
    tables = lax.all_to_all(copies, everywhere, 0, 0, tiled=True)
    row_share = weight.shape[0] // lax.axis_size("pop")
    at = lax.axis_index("pop").astype(jnp.int32).reshape(1)
    estimate, fitness = finish(
        at, tables, seat.astype(jnp.float32), factor_left, factor_right, owned, row_share
    )
    return (estimate, fitness.reshape(owned))


def solution(mesh):
    placed = (P(None, "mp"), P("pop", "mp"), P("pop", "mp"), P(), P(None, "mp"), P("pop"))
    return jax.shard_map(
        per_device,
        mesh=mesh,
        in_specs=placed,
        out_specs=(P("pop", "mp"), P("pop")),
        check_vma=False,
    )
```

```python
import functools
import math

import jax
import jax.numpy as jnp
from jax import lax
from jax.experimental import pallas as pl
from jax.experimental.pallas import tpu as pltpu
from jax.sharding import PartitionSpec as P

D = 4096
FF = 16384
TOK = 128
SIDE = 4
STEPS = (0, 1, -1, 2)

perturb_scale = 0.25
epsilon = 1e-05

COLS = 256
LANES = 128
FEW = 2
VMEM_LIMITS = (26 << 20, 20 << 20, 20 << 20, 20 << 20)


def shift(piece, dx, dy):
    perm = [
        (x * SIDE + y, ((x + dx) % SIDE) * SIDE + (y + dy) % SIDE)
        for x in range(SIDE)
        for y in range(SIDE)
    ]
    return lax.ppermute(piece, "mp", perm)


def first_ring(piece, along_x):
    step = (lambda a, k: shift(a, k, 0)) if along_x else (lambda a, k: shift(a, 0, k))
    half = piece.shape[0] // 2
    back, ahead = step(piece, 1), step(piece, -1)
    return back, ahead, step(back[:half], 1), step(ahead[half:], -1)


def stage_kernel(terms, slots, started, final, idx_ref, *refs):
    refs = list(refs)
    xs = [[refs.pop(0) for _ in block] for block in terms]
    places = dict.fromkeys(place for block in terms for place in block)
    w_refs = {p: [refs.pop(0) for _ in range(SIDE)] for p in places} if len(places) <= FEW else {}
    w_ref = None if w_refs else refs.pop(0)
    left_ref = refs.pop(0)
    sum_ref, sum_proj_ref = (refs.pop(0), refs.pop(0)) if started else (None, None)
    right_ref = refs.pop(0) if final else None
    cot_refs = [refs.pop(0) for _ in terms] if final else None
    out_ref, proj_ref = refs
    rows, extent = xs[0][0].shape
    width = extent // SIDE
    members = rows // TOK

    def product(b, ref):
        total = None
        for x_ref, place in zip(xs[b], terms[b]):
            if ref is None:
                parts = [part[...] for part in w_refs[place]]
            else:
                parts = [
                    ref[pl.ds(pl.multiple_of(idx_ref[place + k] * width, width), width), :]
                    for k in range(SIDE)
                ]
            part = jnp.dot(
                x_ref[...], jnp.concatenate(parts, axis=0), preferred_element_type=jnp.float32
            )
            total = part if total is None else total + part
        return total

    @pl.when(pl.program_id(0) == 0)
    def _():
        for b in range(len(terms)):
            total = product(b, left_ref)
            if started:
                total += sum_proj_ref[b * rows : (b + 1) * rows, :]
            if not final:
                proj_ref[b * rows : (b + 1) * rows, :] = total
                continue
            for m in range(members):
                slot, local = slots[b] + m, b * members + m
                one = total[m * TOK : (m + 1) * TOK, slot : slot + 1]
                proj_ref[local * TOK : (local + 1) * TOK, :] = jnp.broadcast_to(
                    one * (perturb_scale / math.sqrt(D)), (TOK, LANES)
                )
        if final:
            out_ref[...] = jnp.zeros(out_ref.shape, jnp.float32)

    for b in range(len(terms)):
        base = product(b, w_ref)
        if started:
            base += sum_ref[b * rows : (b + 1) * rows, :]
        if not final:
            out_ref[b * rows : (b + 1) * rows, :] = base
            continue
        for m in range(members):
            slot, local = slots[b] + m, b * members + m
            token = slice(m * TOK, (m + 1) * TOK)
            proj = proj_ref[local * TOK : (local + 1) * TOK, :]
            right = right_ref[slot : slot + 1, :]
            sums = jnp.zeros((1, LANES), jnp.float32)
            for g in range(COLS // LANES):
                cols = slice(g * LANES, (g + 1) * LANES)
                act = jnp.maximum(base[token, cols] + proj * right[:, cols], 0.0)
                term = cot_refs[b][token, cols].astype(jnp.float32) * (act * act)
                sums += jnp.sum(term, axis=0, keepdims=True)
            out_ref[slot : slot + 1, :] += sums


def stage(blocks, idx, weight, left_own, limit, sums=None, score=None, slots=None):
    terms = tuple(tuple(place for _, place in block) for block in blocks)
    rows, extent = blocks[0][0][0].shape
    total = rows * len(blocks)
    depth, columns = weight.shape
    whole = lambda n, idx: (0, 0)
    tile = lambda n, idx: (0, n)
    once = pl.Buffered(1)
    operands = [piece for block in blocks for piece, _ in block]
    in_specs = [pl.BlockSpec((rows, extent), whole, pipeline_mode=once)] * len(operands)
    places = dict.fromkeys(place for block in terms for place in block)
    if len(places) > FEW:
        in_specs.append(pl.BlockSpec((depth, COLS), tile))
        operands.append(weight)
    else:
        for place in places:
            for k in range(SIDE):
                row = functools.partial(lambda at, n, idx: (idx[at], n), place + k)
                in_specs.append(pl.BlockSpec((extent // SIDE, COLS), row))
                operands.append(weight)
    in_specs.append(pl.BlockSpec((depth, LANES), whole, pipeline_mode=once))
    operands.append(left_own)
    block = pl.BlockSpec((total, COLS), tile)
    if sums is not None:
        in_specs += [block, pl.BlockSpec((total, LANES), whole, pipeline_mode=once)]
        operands += list(sums)
    if score is None:
        out_specs, scratch = [block, pl.BlockSpec((total, LANES), whole)], []
        out_shape = [
            jax.ShapeDtypeStruct((total, columns), jnp.float32),
            jax.ShapeDtypeStruct((total, LANES), jnp.float32),
        ]
    else:
        right_own, cot = score
        members = right_own.shape[0]
        in_specs.append(pl.BlockSpec((members, COLS), tile))
        operands.append(right_own)
        for slot in slots:
            in_specs.append(
                pl.BlockSpec((rows, COLS), functools.partial(lambda at, n, idx: (at, n), slot * TOK // rows))
            )
            operands.append(cot)
        out_specs = pl.BlockSpec((members, LANES), whole)
        out_shape = jax.ShapeDtypeStruct((members, LANES), jnp.float32)
        scratch = [pltpu.VMEM((total, LANES), jnp.float32)]
    flops = 2 * sum(len(t) for t in terms) * rows * extent * columns
    return pl.pallas_call(
        functools.partial(stage_kernel, terms, slots, sums is not None, score is not None),
        grid_spec=pltpu.PrefetchScalarGridSpec(
            num_scalar_prefetch=1,
            grid=(columns // COLS,),
            in_specs=in_specs,
            out_specs=out_specs,
            scratch_shapes=scratch,
        ),
        out_shape=out_shape,
        compiler_params=pltpu.CompilerParams(vmem_limit_bytes=limit),
        cost_estimate=pl.CostEstimate(
            flops=flops, bytes_accessed=flops // 256, transcendentals=0
        ),
    )(idx, *operands)


def finish_kernel(owned, at_ref, tables_ref, seat_ref, left_ref, right_ref, est_ref, fit_ref):
    members = tables_ref.shape[1]
    row = jnp.sum(tables_ref[...], axis=0, keepdims=True)
    shape = (members, members)
    same = lax.broadcasted_iota(jnp.int32, shape, 0) == lax.broadcasted_iota(jnp.int32, shape, 1)
    column = jnp.sum(
        jnp.where(same, jnp.broadcast_to(row, shape), 0.0), axis=1, keepdims=True
    )
    fit_ref[...] = jnp.sum(seat_ref[...] * column, axis=0, keepdims=True)[:, :owned]
    average = jnp.sum(row) / members
    variance = jnp.sum(jnp.square(row - average)) / members
    spread = jnp.sqrt(jnp.full((members, 1), variance + epsilon, jnp.float32))
    weights = (column - average) / spread / math.sqrt(members)
    scaled = left_ref[...].astype(jnp.float32) * weights
    high = scaled.astype(jnp.bfloat16)
    rest = scaled - high.astype(jnp.float32)
    middle = rest.astype(jnp.bfloat16)
    low = (rest - middle.astype(jnp.float32)).astype(jnp.bfloat16)
    total = None
    for term in (low, middle, high):
        part = lax.dot_general(
            term, right_ref[...], (((0,), (0,)), ((), ())), preferred_element_type=jnp.float32
        )
        total = part if total is None else total + part
    est_ref[...] = total


def finish(at, tables, seat, factor_left, factor_right, owned, row_share):
    devices, members = tables.shape
    columns = factor_right.shape[1]
    return pl.pallas_call(
        functools.partial(finish_kernel, owned),
        grid_spec=pltpu.PrefetchScalarGridSpec(
            num_scalar_prefetch=1,
            grid=(1,),
            in_specs=[
                pl.BlockSpec((devices, members), lambda n, at: (0, 0)),
                pl.BlockSpec((members, LANES), lambda n, at: (0, 0)),
                pl.BlockSpec((members, row_share), lambda n, at: (0, at[0])),
                pl.BlockSpec((members, columns), lambda n, at: (0, 0)),
            ],
            out_specs=[
                pl.BlockSpec((row_share, columns), lambda n, at: (0, 0)),
                pl.BlockSpec((1, owned), lambda n, at: (0, 0)),
            ],
        ),
        out_shape=[
            jax.ShapeDtypeStruct((row_share, columns), jnp.float32),
            jax.ShapeDtypeStruct((1, owned), jnp.float32),
        ],
        compiler_params=pltpu.CompilerParams(vmem_limit_bytes=VMEM_LIMITS[2]),
    )(at, tables, seat, factor_left, factor_right)


def sources(x_first):
    here = lax.axis_index("mp")
    x, y = here // SIDE, here % SIDE
    steps = jnp.array(STEPS, dtype=jnp.int32)
    if x_first:
        index = ((x - steps[None, :]) % SIDE) * SIDE + (y - steps[:, None]) % SIDE
    else:
        index = ((x - steps[:, None]) % SIDE) * SIDE + (y - steps[None, :]) % SIDE
    return index.reshape(-1).astype(jnp.int32)


def per_device(weight, layer_input, cotangent, factor_left, factor_right, seeds):
    members = factor_left.shape[0]
    owned = seeds.shape[0]
    rows = layer_input.shape[0]
    half = rows // 2
    quarter = rows // 4

    pieces = {True: layer_input[:half], False: layer_input[half:]}
    blocks = {}
    for o in (True, False):
        back, ahead, far0, far1 = first_ring(pieces[o], o)
        blocks[o] = [
            jnp.concatenate([pieces[o][s], back[s], ahead[s], far], axis=1)
            for s, far in ((slice(0, quarter), far0), (slice(quarter, half), far1))
        ]

    slots = jnp.pad(seeds, (0, LANES - owned), constant_values=-1)
    seat = slots[None, :] == jnp.arange(members, dtype=jnp.int32)[:, None]
    picked = seat.astype(jnp.bfloat16)
    contract = (((0,), (0,)), ((), ()))
    left_own = lax.dot_general(
        factor_left, picked, contract, preferred_element_type=jnp.float32
    ).astype(jnp.bfloat16)
    right_own = lax.dot_general(
        picked[:, :owned], factor_right, contract, preferred_element_type=jnp.float32
    )

    both = (True, False)
    idx = jnp.concatenate([sources(o) for o in both])
    tie = lax.optimization_barrier

    def send(piece, o, way):
        return shift(piece, 0, way) if o else shift(piece, way, 0)

    def terms(h, *given):
        return [
            [(arrays[o], base + SIDE * group) for arrays, group in given]
            for base, o in ((0, True), (SIDE * SIDE, False))
        ]

    per = quarter // TOK
    slots = [(h * per, (2 + h) * per) for h in range(2)]
    work = (idx, weight, left_own)
    own = [{o: blocks[o][h] for o in both} for h in range(2)]

    back0 = {o: send(own[0][o], o, 1) for o in both}
    ahead0 = {o: send(own[0][o], o, -1) for o in both}
    far0 = {o: send(back0[o], o, 1) for o in both}
    ahead1 = {}
    for o in both:
        ahead0[o], piece = tie((ahead0[o], own[1][o]))
        ahead1[o] = send(piece, o, -1)
    sums0 = stage(terms(0, (own[0], 0), (back0, 1), (ahead0, 2)), *work, VMEM_LIMITS[0])
    far1, back1 = {}, {}
    for o in both:
        ahead1[o], _ = tie((ahead1[o], sums0))
        far1[o] = send(ahead1[o], o, -1)
        far0[o], piece, _ = tie((far0[o], own[1][o], sums0))
        back1[o] = send(piece, o, 1)
    score = (right_own, cotangent)
    scores0 = stage(terms(0, (far0, 3)), *work, VMEM_LIMITS[1], sums0, score, slots[0])
    sums1 = stage(terms(1, (own[1], 0), (ahead1, 2)), *work, VMEM_LIMITS[2])
    scores1 = stage(
        terms(1, (back1, 1), (far1, 3)), *work, VMEM_LIMITS[3], sums1, score, slots[1]
    )
    scores = scores0 + scores1
    partial = -jnp.sum(scores, axis=1) / math.sqrt(TOK * FF)
    seated = seat[:, :owned].astype(jnp.float32)
    table = jnp.sum(seated * partial[None, :], 1)

    everywhere = ("pop", "mp")
    devices = lax.axis_size("pop") * lax.axis_size("mp")
    copies = jnp.broadcast_to(table[None, :], (devices, members))
    tables = lax.all_to_all(copies, everywhere, 0, 0, tiled=True)
    row_share = weight.shape[0] // lax.axis_size("pop")
    at = lax.axis_index("pop").astype(jnp.int32).reshape(1)
    estimate, fitness = finish(
        at, tables, seat.astype(jnp.float32), factor_left, factor_right, owned, row_share
    )
    return (estimate, fitness.reshape(owned))


def solution(mesh):
    placed = (P(None, "mp"), P("pop", "mp"), P("pop", "mp"), P(), P(None, "mp"), P("pop"))
    return jax.shard_map(
        per_device,
        mesh=mesh,
        in_specs=placed,
        out_specs=(P("pop", "mp"), P("pop")),
        check_vma=False,
    )
```

```python
import functools
import math

import jax
import jax.numpy as jnp
from jax import lax
from jax.experimental import pallas as pl
from jax.experimental.pallas import tpu as pltpu
from jax.sharding import PartitionSpec as P

D = 4096
FF = 16384
TOK = 128
SIDE = 4
STEPS = (0, 1, -1, 2)

perturb_scale = 0.25
epsilon = 1e-05

COLS = 256
LANES = 128
VMEM_LIMITS = (36 << 20, 26 << 20, 20 << 20)


def shift(piece, dx, dy):
    perm = [
        (x * SIDE + y, ((x + dx) % SIDE) * SIDE + (y + dy) % SIDE)
        for x in range(SIDE)
        for y in range(SIDE)
    ]
    return lax.ppermute(piece, "mp", perm)


def first_ring(piece, along_x):
    step = (lambda a, k: shift(a, k, 0)) if along_x else (lambda a, k: shift(a, 0, k))
    half = piece.shape[0] // 2
    back, ahead = step(piece, 1), step(piece, -1)
    return back, ahead, step(back[:half], 1), step(ahead[half:], -1)


def stage_kernel(terms, started, final, idx_ref, *refs):
    refs = list(refs)
    xs = [[refs.pop(0) for _ in block] for block in terms]
    w_ref, left_ref = refs.pop(0), refs.pop(0)
    sum_ref, sum_proj_ref = (refs.pop(0), refs.pop(0)) if started else (None, None)
    right_ref, cot_ref = (refs.pop(0), refs.pop(0)) if final else (None, None)
    out_ref, proj_ref = refs
    rows, extent = xs[0][0].shape
    width = extent // SIDE
    members = rows // TOK

    def product(b, ref):
        total = None
        for x_ref, place in zip(xs[b], terms[b]):
            parts = [
                ref[pl.ds(pl.multiple_of(idx_ref[place + k] * width, width), width), :]
                for k in range(SIDE)
            ]
            part = jnp.dot(
                x_ref[...], jnp.concatenate(parts, axis=0), preferred_element_type=jnp.float32
            )
            total = part if total is None else total + part
        return total

    @pl.when(pl.program_id(0) == 0)
    def _():
        for b in range(len(terms)):
            total = product(b, left_ref)
            if started:
                total += sum_proj_ref[b * rows : (b + 1) * rows, :]
            if not final:
                proj_ref[b * rows : (b + 1) * rows, :] = total
                continue
            for m in range(members):
                slot = b * members + m
                one = total[m * TOK : (m + 1) * TOK, slot : slot + 1]
                proj_ref[slot * TOK : (slot + 1) * TOK, :] = jnp.broadcast_to(
                    one * (perturb_scale / math.sqrt(D)), (TOK, LANES)
                )
        if final:
            out_ref[...] = jnp.zeros(out_ref.shape, jnp.float32)

    here = pl.ds(pl.multiple_of(pl.program_id(0) * COLS, COLS), COLS) if final else slice(None)
    for b in range(len(terms)):
        base = product(b, w_ref)
        if started:
            base += sum_ref[b * rows : (b + 1) * rows, here]
        if not final:
            out_ref[b * rows : (b + 1) * rows, :] = base
            continue
        for m in range(members):
            slot = b * members + m
            token = slice(m * TOK, (m + 1) * TOK)
            there = slice(slot * TOK, (slot + 1) * TOK)
            proj = proj_ref[there, :]
            right = right_ref[slot : slot + 1, here]
            cot = cot_ref[there, here].astype(jnp.float32)
            sums = jnp.zeros((1, LANES), jnp.float32)
            for g in range(COLS // LANES):
                cols = slice(g * LANES, (g + 1) * LANES)
                act = jnp.maximum(base[token, cols] + proj * right[:, cols], 0.0)
                term = cot[:, cols] * (act * act)
                sums += jnp.sum(term, axis=0, keepdims=True)
            out_ref[slot : slot + 1, :] += sums


def stage(blocks, idx, weight, left_own, limit, sums=None, score=None):
    terms = tuple(tuple(place for _, place in block) for block in blocks)
    rows, extent = blocks[0][0][0].shape
    total = rows * len(blocks)
    depth, columns = weight.shape
    whole = lambda n, idx: (0, 0)
    tile = lambda n, idx: (0, n)
    once = pl.Buffered(1)
    operands = [piece for block in blocks for piece, _ in block]
    placed = pl.BlockSpec(memory_space=pltpu.VMEM)
    final = score is not None
    in_specs = [
        placed if final else pl.BlockSpec((rows, extent), whole, pipeline_mode=once)
    ] * len(operands)
    in_specs += [
        pl.BlockSpec((depth, COLS), tile),
        placed if final else pl.BlockSpec((depth, LANES), whole, pipeline_mode=once),
    ]
    operands += [weight, left_own]
    block = pl.BlockSpec((total, COLS), tile)
    if sums is not None:
        carried = [block, pl.BlockSpec((total, LANES), whole, pipeline_mode=once)]
        in_specs += [placed, placed] if final else carried
        operands += list(sums)
    if score is None:
        out_specs, scratch = [block, pl.BlockSpec((total, LANES), whole)], []
        out_shape = [
            jax.ShapeDtypeStruct((total, columns), jnp.float32),
            jax.ShapeDtypeStruct((total, LANES), jnp.float32),
        ]
    else:
        members = total // TOK
        in_specs += [placed, placed]
        operands += list(score)
        out_specs = pl.BlockSpec((members, LANES), whole)
        out_shape = jax.ShapeDtypeStruct((members, LANES), jnp.float32)
        scratch = [pltpu.VMEM((total, LANES), jnp.float32)]
    flops = 2 * sum(len(t) for t in terms) * rows * extent * columns
    return pl.pallas_call(
        functools.partial(stage_kernel, terms, sums is not None, score is not None),
        grid_spec=pltpu.PrefetchScalarGridSpec(
            num_scalar_prefetch=1,
            grid=(columns // COLS,),
            in_specs=in_specs,
            out_specs=out_specs,
            scratch_shapes=scratch,
        ),
        out_shape=out_shape,
        compiler_params=pltpu.CompilerParams(vmem_limit_bytes=limit),
        cost_estimate=pl.CostEstimate(
            flops=flops, bytes_accessed=flops // 256, transcendentals=0
        ),
    )(idx, *operands)


def finish_kernel(owned, at_ref, tables_ref, seat_ref, left_ref, right_ref, est_ref, fit_ref):
    members = tables_ref.shape[1]
    row = jnp.sum(tables_ref[...], axis=0, keepdims=True)
    shape = (members, members)
    same = lax.broadcasted_iota(jnp.int32, shape, 0) == lax.broadcasted_iota(jnp.int32, shape, 1)
    column = jnp.sum(
        jnp.where(same, jnp.broadcast_to(row, shape), 0.0), axis=1, keepdims=True
    )
    fit_ref[...] = jnp.sum(seat_ref[...] * column, axis=0, keepdims=True)[:, :owned]
    average = jnp.sum(row) / members
    variance = jnp.sum(jnp.square(row - average)) / members
    spread = jnp.sqrt(jnp.full((members, 1), variance + epsilon, jnp.float32))
    weights = (column - average) / spread / math.sqrt(members)
    scaled = left_ref[...].astype(jnp.float32) * weights
    high = scaled.astype(jnp.bfloat16)
    rest = scaled - high.astype(jnp.float32)
    middle = rest.astype(jnp.bfloat16)
    low = (rest - middle.astype(jnp.float32)).astype(jnp.bfloat16)
    total = None
    for term in (low, middle, high):
        part = lax.dot_general(
            term, right_ref[...], (((0,), (0,)), ((), ())), preferred_element_type=jnp.float32
        )
        total = part if total is None else total + part
    est_ref[...] = total


def finish(at, tables, seat, factor_left, factor_right, owned, row_share):
    devices, members = tables.shape
    columns = factor_right.shape[1]
    return pl.pallas_call(
        functools.partial(finish_kernel, owned),
        grid_spec=pltpu.PrefetchScalarGridSpec(
            num_scalar_prefetch=1,
            grid=(1,),
            in_specs=[
                pl.BlockSpec((devices, members), lambda n, at: (0, 0)),
                pl.BlockSpec((members, LANES), lambda n, at: (0, 0)),
                pl.BlockSpec((members, row_share), lambda n, at: (0, at[0])),
                pl.BlockSpec((members, columns), lambda n, at: (0, 0)),
            ],
            out_specs=[
                pl.BlockSpec((row_share, columns), lambda n, at: (0, 0)),
                pl.BlockSpec((1, owned), lambda n, at: (0, 0)),
            ],
        ),
        out_shape=[
            jax.ShapeDtypeStruct((row_share, columns), jnp.float32),
            jax.ShapeDtypeStruct((1, owned), jnp.float32),
        ],
        compiler_params=pltpu.CompilerParams(vmem_limit_bytes=VMEM_LIMITS[2]),
    )(at, tables, seat, factor_left, factor_right)


def sources(x_first):
    here = lax.axis_index("mp")
    x, y = here // SIDE, here % SIDE
    steps = jnp.array(STEPS, dtype=jnp.int32)
    if x_first:
        index = ((x - steps[None, :]) % SIDE) * SIDE + (y - steps[:, None]) % SIDE
    else:
        index = ((x - steps[:, None]) % SIDE) * SIDE + (y - steps[None, :]) % SIDE
    return index.reshape(-1).astype(jnp.int32)


def per_device(weight, layer_input, cotangent, factor_left, factor_right, seeds):
    members = factor_left.shape[0]
    owned = seeds.shape[0]
    rows = layer_input.shape[0]
    half = rows // 2
    quarter = rows // 4

    pieces = {True: layer_input[:half], False: layer_input[half:]}
    blocks = {}
    for o in (True, False):
        back, ahead, far0, far1 = first_ring(pieces[o], o)
        blocks[o] = [
            jnp.concatenate([pieces[o][s], back[s], ahead[s], far], axis=1)
            for s, far in ((slice(0, quarter), far0), (slice(quarter, half), far1))
        ]

    slots = jnp.pad(seeds, (0, LANES - owned), constant_values=-1)
    seat = slots[None, :] == jnp.arange(members, dtype=jnp.int32)[:, None]
    picked = seat.astype(jnp.bfloat16)
    contract = (((0,), (0,)), ((), ()))
    left_own = lax.dot_general(
        factor_left, picked, contract, preferred_element_type=jnp.float32
    ).astype(jnp.bfloat16)
    right_own = lax.dot_general(
        picked[:, :owned], factor_right, contract, preferred_element_type=jnp.float32
    )

    both = (True, False)
    ways = (1, -1)
    idx = jnp.concatenate([sources(o) for o in both])

    def send(arrays, o, sense):
        return [
            shift(a, 0, sense * way) if o else shift(a, sense * way, 0)
            for a, way in zip(arrays, ways)
        ]

    def terms(*given):
        out = []
        for base, o in ((0, True), (SIDE * SIDE, False)):
            for h in range(2):
                out.append([(arrays[o][h], base + SIDE * groups[h]) for arrays, groups in given])
        return out

    near = {o: send(blocks[o], o, 1) for o in both}
    far = {o: send(near[o], o, 1) for o in both}
    sums = stage(terms((blocks, (0, 0)), (near, (1, 2))), idx, weight, left_own, VMEM_LIMITS[0])
    far, sums, blocks = lax.optimization_barrier((far, sums, blocks))
    other = {o: send(blocks[o], o, -1) for o in both}
    sums = stage(terms((far, (3, 3))), idx, weight, left_own, VMEM_LIMITS[1], sums)
    scores = stage(
        terms((other, (2, 1))), idx, weight, left_own, VMEM_LIMITS[2], sums, (right_own, cotangent)
    )
    partial = -jnp.sum(scores, axis=1) / math.sqrt(TOK * FF)
    seated = seat[:, :owned].astype(jnp.float32)
    table = jnp.sum(seated * partial[None, :], 1)

    everywhere = ("pop", "mp")
    devices = lax.axis_size("pop") * lax.axis_size("mp")
    copies = jnp.broadcast_to(table[None, :], (devices, members))
    tables = lax.all_to_all(copies, everywhere, 0, 0, tiled=True)
    row_share = weight.shape[0] // lax.axis_size("pop")
    at = lax.axis_index("pop").astype(jnp.int32).reshape(1)
    estimate, fitness = finish(
        at, tables, seat.astype(jnp.float32), factor_left, factor_right, owned, row_share
    )
    return (estimate, fitness.reshape(owned))


def solution(mesh):
    placed = (P(None, "mp"), P("pop", "mp"), P("pop", "mp"), P(), P(None, "mp"), P("pop"))
    return jax.shard_map(
        per_device,
        mesh=mesh,
        in_specs=placed,
        out_specs=(P("pop", "mp"), P("pop")),
        check_vma=False,
    )
```

```python
import functools
import math

import jax
import jax.numpy as jnp
from jax import lax
from jax.experimental import pallas as pl
from jax.experimental.pallas import tpu as pltpu
from jax.sharding import PartitionSpec as P

D = 4096
FF = 16384
TOK = 128
SIDE = 4
STEPS = (0, 1, -1, 2)

perturb_scale = 0.25
epsilon = 1e-05

COLS = 256
LANES = 128
VMEM_LIMITS = (36 << 20, 26 << 20, 20 << 20)


def shift(piece, dx, dy):
    perm = [
        (x * SIDE + y, ((x + dx) % SIDE) * SIDE + (y + dy) % SIDE)
        for x in range(SIDE)
        for y in range(SIDE)
    ]
    return lax.ppermute(piece, "mp", perm)


def first_ring(piece, along_x):
    step = (lambda a, k: shift(a, k, 0)) if along_x else (lambda a, k: shift(a, 0, k))
    half = piece.shape[0] // 2
    back, ahead = step(piece, 1), step(piece, -1)
    return back, ahead, step(back[:half], 1), step(ahead[half:], -1)


def stage_kernel(terms, started, final, idx_ref, *refs):
    refs = list(refs)
    xs = [[refs.pop(0) for _ in block] for block in terms]
    w_ref, left_ref = refs.pop(0), refs.pop(0)
    sum_ref, sum_proj_ref = (refs.pop(0), refs.pop(0)) if started else (None, None)
    right_ref, cot_ref, seat_ref = [refs.pop(0) for _ in range(3)] if final else [None] * 3
    if final:
        table_ref, proj_ref, out_ref = refs
    else:
        out_ref, proj_ref = refs
    rows, extent = xs[0][0].shape
    width = extent // SIDE
    members = rows // TOK

    def product(b, ref):
        total = None
        for x_ref, place in zip(xs[b], terms[b]):
            parts = [
                ref[pl.ds(pl.multiple_of(idx_ref[place + k] * width, width), width), :]
                for k in range(SIDE)
            ]
            part = jnp.dot(
                x_ref[...], jnp.concatenate(parts, axis=0), preferred_element_type=jnp.float32
            )
            total = part if total is None else total + part
        return total

    @pl.when(pl.program_id(0) == 0)
    def _():
        for b in range(len(terms)):
            total = product(b, left_ref)
            if started:
                total += sum_proj_ref[b * rows : (b + 1) * rows, :]
            if not final:
                proj_ref[b * rows : (b + 1) * rows, :] = total
                continue
            for m in range(members):
                slot = b * members + m
                one = total[m * TOK : (m + 1) * TOK, slot : slot + 1]
                proj_ref[slot * TOK : (slot + 1) * TOK, :] = jnp.broadcast_to(
                    one * (perturb_scale / math.sqrt(D)), (TOK, LANES)
                )
        if final:
            out_ref[...] = jnp.zeros(out_ref.shape, jnp.float32)

    here = pl.ds(pl.multiple_of(pl.program_id(0) * COLS, COLS), COLS) if final else slice(None)
    for b in range(len(terms)):
        base = product(b, w_ref)
        if started:
            base += sum_ref[b * rows : (b + 1) * rows, here]
        if not final:
            out_ref[b * rows : (b + 1) * rows, :] = base
            continue
        for m in range(members):
            slot = b * members + m
            token = slice(m * TOK, (m + 1) * TOK)
            there = slice(slot * TOK, (slot + 1) * TOK)
            proj = proj_ref[there, :]
            right = right_ref[slot : slot + 1, here]
            cot = cot_ref[there, here].astype(jnp.float32)
            sums = jnp.zeros((1, LANES), jnp.float32)
            for g in range(COLS // LANES):
                cols = slice(g * LANES, (g + 1) * LANES)
                act = jnp.maximum(base[token, cols] + proj * right[:, cols], 0.0)
                term = cot[:, cols] * (act * act)
                sums += jnp.sum(term, axis=0, keepdims=True)
            out_ref[slot : slot + 1, :] += sums

    if final:

        @pl.when(pl.program_id(0) == pl.num_programs(0) - 1)
        def _():
            fitness = jnp.sum(out_ref[...], axis=1, keepdims=True) / -math.sqrt(TOK * FF)
            table = jnp.sum(seat_ref[...] * fitness, axis=0, keepdims=True)
            table_ref[...] = jnp.broadcast_to(table[None], table_ref.shape)


def stage(blocks, idx, weight, left_own, limit, sums=None, score=None):
    terms = tuple(tuple(place for _, place in block) for block in blocks)
    rows, extent = blocks[0][0][0].shape
    total = rows * len(blocks)
    depth, columns = weight.shape
    whole = lambda n, idx: (0, 0)
    tile = lambda n, idx: (0, n)
    once = pl.Buffered(1)
    operands = [piece for block in blocks for piece, _ in block]
    placed = pl.BlockSpec(memory_space=pltpu.VMEM)
    final = score is not None
    in_specs = [
        placed if final else pl.BlockSpec((rows, extent), whole, pipeline_mode=once)
    ] * len(operands)
    in_specs += [
        pl.BlockSpec((depth, COLS), tile),
        placed if final else pl.BlockSpec((depth, LANES), whole, pipeline_mode=once),
    ]
    operands += [weight, left_own]
    block = pl.BlockSpec((total, COLS), tile)
    if sums is not None:
        carried = [block, pl.BlockSpec((total, LANES), whole, pipeline_mode=once)]
        in_specs += [placed, placed] if final else carried
        operands += list(sums)
    if score is None:
        out_specs, scratch = [block, pl.BlockSpec((total, LANES), whole)], []
        out_shape = [
            jax.ShapeDtypeStruct((total, columns), jnp.float32),
            jax.ShapeDtypeStruct((total, LANES), jnp.float32),
        ]
    else:
        members = total // TOK
        in_specs += [placed] * 3
        operands += list(score[:3])
        devices, table = score[3], score[2].shape[1]
        out_specs = pl.BlockSpec((devices, 1, table), lambda n, idx: (0, 0, 0))
        out_shape = jax.ShapeDtypeStruct((devices, 1, table), jnp.float32)
        scratch = [
            pltpu.VMEM((total, LANES), jnp.float32),
            pltpu.VMEM((members, LANES), jnp.float32),
        ]
    flops = 2 * sum(len(t) for t in terms) * rows * extent * columns
    return pl.pallas_call(
        functools.partial(stage_kernel, terms, sums is not None, score is not None),
        grid_spec=pltpu.PrefetchScalarGridSpec(
            num_scalar_prefetch=1,
            grid=(columns // COLS,),
            in_specs=in_specs,
            out_specs=out_specs,
            scratch_shapes=scratch,
        ),
        out_shape=out_shape,
        compiler_params=pltpu.CompilerParams(vmem_limit_bytes=limit),
        cost_estimate=pl.CostEstimate(
            flops=flops, bytes_accessed=flops // 256, transcendentals=0
        ),
    )(idx, *operands)


def finish_kernel(owned, at_ref, tables_ref, seat_ref, left_ref, right_ref, est_ref, fit_ref):
    members = tables_ref.shape[1]
    row = jnp.sum(tables_ref[...], axis=0, keepdims=True)
    shape = (members, members)
    same = lax.broadcasted_iota(jnp.int32, shape, 0) == lax.broadcasted_iota(jnp.int32, shape, 1)
    column = jnp.sum(
        jnp.where(same, jnp.broadcast_to(row, shape), 0.0), axis=1, keepdims=True
    )
    fit_ref[...] = jnp.sum(seat_ref[...] * column, axis=0, keepdims=True)[:, :owned]
    average = jnp.sum(row) / members
    variance = jnp.sum(jnp.square(row - average)) / members
    spread = jnp.sqrt(jnp.full((members, 1), variance + epsilon, jnp.float32))
    weights = (column - average) / spread / math.sqrt(members)
    scaled = left_ref[...].astype(jnp.float32) * weights
    high = scaled.astype(jnp.bfloat16)
    rest = scaled - high.astype(jnp.float32)
    middle = rest.astype(jnp.bfloat16)
    low = (rest - middle.astype(jnp.float32)).astype(jnp.bfloat16)
    total = None
    for term in (low, middle, high):
        part = lax.dot_general(
            term, right_ref[...], (((0,), (0,)), ((), ())), preferred_element_type=jnp.float32
        )
        total = part if total is None else total + part
    est_ref[...] = total


def finish(at, tables, seat, factor_left, factor_right, owned, row_share):
    devices, members = tables.shape
    columns = factor_right.shape[1]
    return pl.pallas_call(
        functools.partial(finish_kernel, owned),
        grid_spec=pltpu.PrefetchScalarGridSpec(
            num_scalar_prefetch=1,
            grid=(1,),
            in_specs=[
                pl.BlockSpec((devices, members), lambda n, at: (0, 0)),
                pl.BlockSpec((members, LANES), lambda n, at: (0, 0)),
                pl.BlockSpec((members, row_share), lambda n, at: (0, at[0])),
                pl.BlockSpec((members, columns), lambda n, at: (0, 0)),
            ],
            out_specs=[
                pl.BlockSpec((row_share, columns), lambda n, at: (0, 0)),
                pl.BlockSpec((1, owned), lambda n, at: (0, 0)),
            ],
        ),
        out_shape=[
            jax.ShapeDtypeStruct((row_share, columns), jnp.float32),
            jax.ShapeDtypeStruct((1, owned), jnp.float32),
        ],
        compiler_params=pltpu.CompilerParams(vmem_limit_bytes=VMEM_LIMITS[2]),
    )(at, tables, seat, factor_left, factor_right)


def sources(x_first):
    here = lax.axis_index("mp")
    x, y = here // SIDE, here % SIDE
    steps = jnp.array(STEPS, dtype=jnp.int32)
    if x_first:
        index = ((x - steps[None, :]) % SIDE) * SIDE + (y - steps[:, None]) % SIDE
    else:
        index = ((x - steps[:, None]) % SIDE) * SIDE + (y - steps[None, :]) % SIDE
    return index.reshape(-1).astype(jnp.int32)


def per_device(weight, layer_input, cotangent, factor_left, factor_right, seeds):
    members = factor_left.shape[0]
    owned = seeds.shape[0]
    rows = layer_input.shape[0]
    half = rows // 2
    quarter = rows // 4

    pieces = {True: layer_input[:half], False: layer_input[half:]}
    blocks = {}
    for o in (True, False):
        back, ahead, far0, far1 = first_ring(pieces[o], o)
        blocks[o] = [
            jnp.concatenate([pieces[o][s], back[s], ahead[s], far], axis=1)
            for s, far in ((slice(0, quarter), far0), (slice(quarter, half), far1))
        ]

    slots = jnp.pad(seeds, (0, LANES - owned), constant_values=-1)
    seat = slots[None, :] == jnp.arange(members, dtype=jnp.int32)[:, None]
    picked = seat.astype(jnp.bfloat16)
    contract = (((0,), (0,)), ((), ()))
    left_own = lax.dot_general(
        factor_left, picked, contract, preferred_element_type=jnp.float32
    ).astype(jnp.bfloat16)
    right_own = lax.dot_general(
        picked[:, :owned], factor_right, contract, preferred_element_type=jnp.float32
    )

    both = (True, False)
    ways = (1, -1)
    idx = jnp.concatenate([sources(o) for o in both])

    def send(arrays, o, sense):
        return [
            shift(a, 0, sense * way) if o else shift(a, sense * way, 0)
            for a, way in zip(arrays, ways)
        ]

    def terms(*given):
        out = []
        for base, o in ((0, True), (SIDE * SIDE, False)):
            for h in range(2):
                out.append([(arrays[o][h], base + SIDE * groups[h]) for arrays, groups in given])
        return out

    near = {o: send(blocks[o], o, 1) for o in both}
    far = {o: send(near[o], o, 1) for o in both}
    sums = stage(terms((blocks, (0, 0)), (near, (1, 2))), idx, weight, left_own, VMEM_LIMITS[0])
    far, sums, blocks = lax.optimization_barrier((far, sums, blocks))
    other = {o: send(blocks[o], o, -1) for o in both}
    sums = stage(terms((far, (3, 3))), idx, weight, left_own, VMEM_LIMITS[1], sums)
    everywhere = ("pop", "mp")
    devices = lax.axis_size("pop") * lax.axis_size("mp")
    seated = (seeds[:, None] == jnp.arange(members, dtype=jnp.int32)[None, :]).astype(jnp.float32)
    copies = stage(
        terms((other, (2, 1))), idx, weight, left_own, VMEM_LIMITS[2], sums,
        (right_own, cotangent, seated, devices),
    )
    tables = lax.all_to_all(copies, everywhere, 0, 0, tiled=True).reshape(devices, members)
    row_share = weight.shape[0] // lax.axis_size("pop")
    at = lax.axis_index("pop").astype(jnp.int32).reshape(1)
    estimate, fitness = finish(
        at, tables, seat.astype(jnp.float32), factor_left, factor_right, owned, row_share
    )
    return (estimate, fitness.reshape(owned))


def solution(mesh):
    placed = (P(None, "mp"), P("pop", "mp"), P("pop", "mp"), P(), P(None, "mp"), P("pop"))
    return jax.shard_map(
        per_device,
        mesh=mesh,
        in_specs=placed,
        out_specs=(P("pop", "mp"), P("pop")),
        check_vma=False,
    )
```

```python
import functools
import math

import jax
import jax.numpy as jnp
from jax import lax
from jax.experimental import pallas as pl
from jax.experimental.pallas import tpu as pltpu
from jax.sharding import PartitionSpec as P

D = 4096
FF = 16384
TOK = 128
SIDE = 4
STEPS = (0, 1, -1, 2)

perturb_scale = 0.25
epsilon = 1e-05

COLS = 256
LANES = 128
VMEM_LIMITS = (36 << 20, 26 << 20, 20 << 20)


def shift(piece, dx, dy):
    perm = [
        (x * SIDE + y, ((x + dx) % SIDE) * SIDE + (y + dy) % SIDE)
        for x in range(SIDE)
        for y in range(SIDE)
    ]
    return lax.ppermute(piece, "mp", perm)


def first_ring(piece, along_x):
    step = (lambda a, k: shift(a, k, 0)) if along_x else (lambda a, k: shift(a, 0, k))
    half = piece.shape[0] // 2
    back, ahead = step(piece, 1), step(piece, -1)
    return back, ahead, step(back[:half], 1), step(ahead[half:], -1)


def stage_kernel(terms, started, final, idx_ref, *refs):
    refs = list(refs)
    xs = [[refs.pop(0) for _ in block] for block in terms]
    w_ref, left_ref = refs.pop(0), refs.pop(0)
    sum_ref, sum_proj_ref = (refs.pop(0), refs.pop(0)) if started else (None, None)
    right_ref, cot_ref, seat_ref = [refs.pop(0) for _ in range(3)] if final else [None] * 3
    if final:
        table_ref, proj_ref, out_ref = refs
    else:
        out_ref, proj_ref = refs
    rows, extent = xs[0][0].shape
    width = extent // SIDE
    members = rows // TOK

    def product(b, ref):
        total = None
        for x_ref, place in zip(xs[b], terms[b]):
            parts = [
                ref[pl.ds(pl.multiple_of(idx_ref[place + k] * width, width), width), :]
                for k in range(SIDE)
            ]
            part = jnp.dot(
                x_ref[...], jnp.concatenate(parts, axis=0), preferred_element_type=jnp.float32
            )
            total = part if total is None else total + part
        return total

    @pl.when(pl.program_id(0) == 0)
    def _():
        for b in range(len(terms)):
            total = product(b, left_ref)
            if started:
                total += sum_proj_ref[b * rows : (b + 1) * rows, :]
            if not final:
                proj_ref[b * rows : (b + 1) * rows, :] = total
                continue
            for m in range(members):
                slot = b * members + m
                one = total[m * TOK : (m + 1) * TOK, slot : slot + 1]
                proj_ref[slot * TOK : (slot + 1) * TOK, :] = jnp.broadcast_to(
                    one * (perturb_scale / math.sqrt(D)), (TOK, LANES)
                )
        if final:
            out_ref[...] = jnp.zeros(out_ref.shape, jnp.float32)

    here = pl.ds(pl.multiple_of(pl.program_id(0) * COLS, COLS), COLS) if final else slice(None)
    ahead = product(0, w_ref)
    for b in range(len(terms)):
        base = ahead
        if b + 1 < len(terms):
            ahead = product(b + 1, w_ref)
        if started and not final:
            base += sum_ref[b * rows : (b + 1) * rows, here]
        if not final:
            out_ref[b * rows : (b + 1) * rows, :] = base
            continue
        for m in range(members):
            slot = b * members + m
            token = slice(m * TOK, (m + 1) * TOK)
            there = slice(slot * TOK, (slot + 1) * TOK)
            proj = proj_ref[there, :]
            right = right_ref[slot : slot + 1, here]
            cot = cot_ref[there, here].astype(jnp.float32)
            carried = sum_ref[there, here]
            sums = jnp.zeros((1, LANES), jnp.float32)
            for g in range(COLS // LANES):
                cols = slice(g * LANES, (g + 1) * LANES)
                rest = carried[:, cols] + proj * right[:, cols]
                act = jnp.maximum(base[token, cols] + rest, 0.0)
                term = cot[:, cols] * (act * act)
                sums += jnp.sum(term, axis=0, keepdims=True)
            out_ref[slot : slot + 1, :] += sums

    if final:

        @pl.when(pl.program_id(0) == pl.num_programs(0) - 1)
        def _():
            fitness = jnp.sum(out_ref[...], axis=1, keepdims=True) / -math.sqrt(TOK * FF)
            table = jnp.sum(seat_ref[...] * fitness, axis=0, keepdims=True)
            table_ref[...] = jnp.broadcast_to(table[None], table_ref.shape)


def stage(blocks, idx, weight, left_own, limit, sums=None, score=None):
    terms = tuple(tuple(place for _, place in block) for block in blocks)
    rows, extent = blocks[0][0][0].shape
    total = rows * len(blocks)
    depth, columns = weight.shape
    whole = lambda n, idx: (0, 0)
    tile = lambda n, idx: (0, n)
    once = pl.Buffered(1)
    operands = [piece for block in blocks for piece, _ in block]
    placed = pl.BlockSpec(memory_space=pltpu.VMEM)
    final = score is not None
    in_specs = [
        placed if final else pl.BlockSpec((rows, extent), whole, pipeline_mode=once)
    ] * len(operands)
    in_specs += [
        pl.BlockSpec((depth, COLS), tile),
        placed if final else pl.BlockSpec((depth, LANES), whole, pipeline_mode=once),
    ]
    operands += [weight, left_own]
    block = pl.BlockSpec((total, COLS), tile)
    if sums is not None:
        carried = [block, pl.BlockSpec((total, LANES), whole, pipeline_mode=once)]
        in_specs += [placed, placed] if final else carried
        operands += list(sums)
    if score is None:
        out_specs, scratch = [block, pl.BlockSpec((total, LANES), whole)], []
        out_shape = [
            jax.ShapeDtypeStruct((total, columns), jnp.float32),
            jax.ShapeDtypeStruct((total, LANES), jnp.float32),
        ]
    else:
        members = total // TOK
        in_specs += [placed] * 3
        operands += list(score[:3])
        devices, table = score[3], score[2].shape[1]
        out_specs = pl.BlockSpec((devices, 1, table), lambda n, idx: (0, 0, 0))
        out_shape = jax.ShapeDtypeStruct((devices, 1, table), jnp.float32)
        scratch = [
            pltpu.VMEM((total, LANES), jnp.float32),
            pltpu.VMEM((members, LANES), jnp.float32),
        ]
    flops = 2 * sum(len(t) for t in terms) * rows * extent * columns
    return pl.pallas_call(
        functools.partial(stage_kernel, terms, sums is not None, score is not None),
        grid_spec=pltpu.PrefetchScalarGridSpec(
            num_scalar_prefetch=1,
            grid=(columns // COLS,),
            in_specs=in_specs,
            out_specs=out_specs,
            scratch_shapes=scratch,
        ),
        out_shape=out_shape,
        compiler_params=pltpu.CompilerParams(vmem_limit_bytes=limit),
        cost_estimate=pl.CostEstimate(
            flops=flops, bytes_accessed=flops // 256, transcendentals=0
        ),
    )(idx, *operands)


def finish_kernel(owned, at_ref, tables_ref, seat_ref, left_ref, right_ref, est_ref, fit_ref):
    members = tables_ref.shape[1]
    row = jnp.sum(tables_ref[...], axis=0, keepdims=True)
    shape = (members, members)
    same = lax.broadcasted_iota(jnp.int32, shape, 0) == lax.broadcasted_iota(jnp.int32, shape, 1)
    column = jnp.sum(
        jnp.where(same, jnp.broadcast_to(row, shape), 0.0), axis=1, keepdims=True
    )
    fit_ref[...] = jnp.sum(seat_ref[...] * column, axis=0, keepdims=True)[:, :owned]
    average = jnp.sum(row) / members
    variance = jnp.sum(jnp.square(row - average)) / members
    spread = jnp.sqrt(jnp.full((members, 1), variance + epsilon, jnp.float32))
    weights = (column - average) / spread / math.sqrt(members)
    scaled = left_ref[...].astype(jnp.float32) * weights
    high = scaled.astype(jnp.bfloat16)
    rest = scaled - high.astype(jnp.float32)
    middle = rest.astype(jnp.bfloat16)
    low = (rest - middle.astype(jnp.float32)).astype(jnp.bfloat16)
    total = None
    for term in (low, middle, high):
        part = lax.dot_general(
            term, right_ref[...], (((0,), (0,)), ((), ())), preferred_element_type=jnp.float32
        )
        total = part if total is None else total + part
    est_ref[...] = total


def finish(at, tables, seat, factor_left, factor_right, owned, row_share):
    devices, members = tables.shape
    columns = factor_right.shape[1]
    return pl.pallas_call(
        functools.partial(finish_kernel, owned),
        grid_spec=pltpu.PrefetchScalarGridSpec(
            num_scalar_prefetch=1,
            grid=(1,),
            in_specs=[
                pl.BlockSpec((devices, members), lambda n, at: (0, 0)),
                pl.BlockSpec((members, LANES), lambda n, at: (0, 0)),
                pl.BlockSpec((members, row_share), lambda n, at: (0, at[0])),
                pl.BlockSpec((members, columns), lambda n, at: (0, 0)),
            ],
            out_specs=[
                pl.BlockSpec((row_share, columns), lambda n, at: (0, 0)),
                pl.BlockSpec((1, owned), lambda n, at: (0, 0)),
            ],
        ),
        out_shape=[
            jax.ShapeDtypeStruct((row_share, columns), jnp.float32),
            jax.ShapeDtypeStruct((1, owned), jnp.float32),
        ],
        compiler_params=pltpu.CompilerParams(vmem_limit_bytes=VMEM_LIMITS[2]),
    )(at, tables, seat, factor_left, factor_right)


def sources(x_first):
    here = lax.axis_index("mp")
    x, y = here // SIDE, here % SIDE
    steps = jnp.array(STEPS, dtype=jnp.int32)
    if x_first:
        index = ((x - steps[None, :]) % SIDE) * SIDE + (y - steps[:, None]) % SIDE
    else:
        index = ((x - steps[:, None]) % SIDE) * SIDE + (y - steps[None, :]) % SIDE
    return index.reshape(-1).astype(jnp.int32)


def per_device(weight, layer_input, cotangent, factor_left, factor_right, seeds):
    members = factor_left.shape[0]
    owned = seeds.shape[0]
    rows = layer_input.shape[0]
    half = rows // 2
    quarter = rows // 4

    pieces = {True: layer_input[:half], False: layer_input[half:]}
    blocks = {}
    for o in (True, False):
        back, ahead, far0, far1 = first_ring(pieces[o], o)
        blocks[o] = [
            jnp.concatenate([pieces[o][s], back[s], ahead[s], far], axis=1)
            for s, far in ((slice(0, quarter), far0), (slice(quarter, half), far1))
        ]

    slots = jnp.pad(seeds, (0, LANES - owned), constant_values=-1)
    seat = slots[None, :] == jnp.arange(members, dtype=jnp.int32)[:, None]
    picked = seat.astype(jnp.bfloat16)
    contract = (((0,), (0,)), ((), ()))
    left_own = lax.dot_general(
        factor_left, picked, contract, preferred_element_type=jnp.float32
    ).astype(jnp.bfloat16)
    right_own = lax.dot_general(
        picked[:, :owned], factor_right, contract, preferred_element_type=jnp.float32
    )

    both = (True, False)
    ways = (1, -1)
    idx = jnp.concatenate([sources(o) for o in both])

    def send(arrays, o, sense):
        return [
            shift(a, 0, sense * way) if o else shift(a, sense * way, 0)
            for a, way in zip(arrays, ways)
        ]

    def terms(*given):
        out = []
        for base, o in ((0, True), (SIDE * SIDE, False)):
            for h in range(2):
                out.append([(arrays[o][h], base + SIDE * groups[h]) for arrays, groups in given])
        return out

    near = {o: send(blocks[o], o, 1) for o in both}
    far = {o: send(near[o], o, 1) for o in both}
    sums = stage(terms((blocks, (0, 0)), (near, (1, 2))), idx, weight, left_own, VMEM_LIMITS[0])
    far, sums, blocks = lax.optimization_barrier((far, sums, blocks))
    other = {o: send(blocks[o], o, -1) for o in both}
    sums = stage(terms((far, (3, 3))), idx, weight, left_own, VMEM_LIMITS[1], sums)
    everywhere = ("pop", "mp")
    devices = lax.axis_size("pop") * lax.axis_size("mp")
    seated = (seeds[:, None] == jnp.arange(members, dtype=jnp.int32)[None, :]).astype(jnp.float32)
    copies = stage(
        terms((other, (2, 1))), idx, weight, left_own, VMEM_LIMITS[2], sums,
        (right_own, cotangent, seated, devices),
    )
    tables = lax.all_to_all(copies, everywhere, 0, 0, tiled=True).reshape(devices, members)
    row_share = weight.shape[0] // lax.axis_size("pop")
    at = lax.axis_index("pop").astype(jnp.int32).reshape(1)
    estimate, fitness = finish(
        at, tables, seat.astype(jnp.float32), factor_left, factor_right, owned, row_share
    )
    return (estimate, fitness.reshape(owned))


def solution(mesh):
    placed = (P(None, "mp"), P("pop", "mp"), P("pop", "mp"), P(), P(None, "mp"), P("pop"))
    return jax.shard_map(
        per_device,
        mesh=mesh,
        in_specs=placed,
        out_specs=(P("pop", "mp"), P("pop")),
        check_vma=False,
    )
```

```python
import functools
import math

import jax
import jax.numpy as jnp
from jax import lax
from jax.experimental import pallas as pl
from jax.experimental.pallas import tpu as pltpu
from jax.sharding import PartitionSpec as P

D = 4096
FF = 16384
TOK = 128
SIDE = 4
STEPS = (0, 1, -1, 2)

perturb_scale = 0.25
epsilon = 1e-05

COLS = 256
LANES = 128
VMEM_LIMITS = (50 << 20, 26 << 20, 16 << 20)


def shift(piece, dx, dy):
    perm = [
        (x * SIDE + y, ((x + dx) % SIDE) * SIDE + (y + dy) % SIDE)
        for x in range(SIDE)
        for y in range(SIDE)
    ]
    return lax.ppermute(piece, "mp", perm)


def first_ring(piece, along_x):
    step = (lambda a, k: shift(a, k, 0)) if along_x else (lambda a, k: shift(a, 0, k))
    half = piece.shape[0] // 2
    back, ahead = step(piece, 1), step(piece, -1)
    return back, ahead, step(back[:half], 1), step(ahead[half:], -1)


def stage_kernel(terms, started, final, idx_ref, *refs):
    refs = list(refs)
    xs = [[refs.pop(0) for _ in block] for block in terms]
    w_ref, left_ref = refs.pop(0), refs.pop(0)
    sum_ref, sum_proj_ref = (refs.pop(0), refs.pop(0)) if started else (None, None)
    right_ref, cot_ref, seat_ref = [refs.pop(0) for _ in range(3)] if final else [None] * 3
    if final:
        table_ref, proj_ref, out_ref = refs
    else:
        out_ref, proj_ref = refs
    rows, extent = xs[0][0].shape
    width = extent // SIDE
    members = rows // TOK

    def product(b, ref):
        total = None
        for x_ref, place in zip(xs[b], terms[b]):
            parts = [
                ref[pl.ds(pl.multiple_of(idx_ref[place + k] * width, width), width), :]
                for k in range(SIDE)
            ]
            part = jnp.dot(
                x_ref[...], jnp.concatenate(parts, axis=0), preferred_element_type=jnp.float32
            )
            total = part if total is None else total + part
        return total

    @pl.when(pl.program_id(0) == 0)
    def _():
        for b in range(len(terms)):
            total = product(b, left_ref)
            if started:
                total += sum_proj_ref[b * rows : (b + 1) * rows, :]
            if not final:
                proj_ref[b * rows : (b + 1) * rows, :] = total
                continue
            for m in range(members):
                slot = b * members + m
                one = total[m * TOK : (m + 1) * TOK, slot : slot + 1]
                proj_ref[slot * TOK : (slot + 1) * TOK, :] = jnp.broadcast_to(
                    one * (perturb_scale / math.sqrt(D)), (TOK, LANES)
                )
        if final:
            out_ref[...] = jnp.zeros(out_ref.shape, jnp.float32)

    here = pl.ds(pl.multiple_of(pl.program_id(0) * COLS, COLS), COLS) if final else slice(None)
    ahead = product(0, w_ref)
    for b in range(len(terms)):
        base = ahead
        if b + 1 < len(terms):
            ahead = product(b + 1, w_ref)
        if started and not final:
            base += sum_ref[b * rows : (b + 1) * rows, here]
        if not final:
            out_ref[b * rows : (b + 1) * rows, :] = base
            continue
        for m in range(members):
            slot = b * members + m
            token = slice(m * TOK, (m + 1) * TOK)
            there = slice(slot * TOK, (slot + 1) * TOK)
            proj = proj_ref[there, :]
            right = right_ref[slot : slot + 1, here]
            cot = cot_ref[there, here].astype(jnp.float32)
            carried = sum_ref[there, here]
            sums = jnp.zeros((1, LANES), jnp.float32)
            for g in range(COLS // LANES):
                cols = slice(g * LANES, (g + 1) * LANES)
                rest = carried[:, cols] + proj * right[:, cols]
                act = jnp.maximum(base[token, cols] + rest, 0.0)
                term = cot[:, cols] * (act * act)
                sums += jnp.sum(term, axis=0, keepdims=True)
            out_ref[slot : slot + 1, :] += sums

    if final:

        @pl.when(pl.program_id(0) == pl.num_programs(0) - 1)
        def _():
            fitness = jnp.sum(out_ref[...], axis=1, keepdims=True) / -math.sqrt(TOK * FF)
            table = jnp.sum(seat_ref[...] * fitness, axis=0, keepdims=True)
            table_ref[...] = jnp.broadcast_to(table[None], table_ref.shape)


def stage(blocks, idx, weight, left_own, limit, sums=None, score=None):
    terms = tuple(tuple(place for _, place in block) for block in blocks)
    rows, extent = blocks[0][0][0].shape
    total = rows * len(blocks)
    depth, columns = weight.shape
    whole = lambda n, idx: (0, 0)
    tile = lambda n, idx: (0, n)
    once = pl.Buffered(1)
    operands = [piece for block in blocks for piece, _ in block]
    placed = pl.BlockSpec(memory_space=pltpu.VMEM)
    final = score is not None
    in_specs = [
        placed if final else pl.BlockSpec((rows, extent), whole, pipeline_mode=once)
    ] * len(operands)
    in_specs += [
        pl.BlockSpec((depth, COLS), tile),
        placed if final else pl.BlockSpec((depth, LANES), whole, pipeline_mode=once),
    ]
    operands += [weight, left_own]
    block = pl.BlockSpec((total, COLS), tile)
    if sums is not None:
        carried = [block, pl.BlockSpec((total, LANES), whole, pipeline_mode=once)]
        in_specs += [placed, placed] if final else carried
        operands += list(sums)
    if score is None:
        out_specs, scratch = [block, pl.BlockSpec((total, LANES), whole)], []
        out_shape = [
            jax.ShapeDtypeStruct((total, columns), jnp.float32),
            jax.ShapeDtypeStruct((total, LANES), jnp.float32),
        ]
    else:
        members = total // TOK
        in_specs += [placed] * 3
        operands += list(score[:3])
        devices, table = score[3], score[2].shape[1]
        out_specs = pl.BlockSpec((devices, 1, table), lambda n, idx: (0, 0, 0))
        out_shape = jax.ShapeDtypeStruct((devices, 1, table), jnp.float32)
        scratch = [
            pltpu.VMEM((total, LANES), jnp.float32),
            pltpu.VMEM((members, LANES), jnp.float32),
        ]
    flops = 2 * sum(len(t) for t in terms) * rows * extent * columns
    return pl.pallas_call(
        functools.partial(stage_kernel, terms, sums is not None, score is not None),
        grid_spec=pltpu.PrefetchScalarGridSpec(
            num_scalar_prefetch=1,
            grid=(columns // COLS,),
            in_specs=in_specs,
            out_specs=out_specs,
            scratch_shapes=scratch,
        ),
        out_shape=out_shape,
        compiler_params=pltpu.CompilerParams(vmem_limit_bytes=limit),
        cost_estimate=pl.CostEstimate(
            flops=flops, bytes_accessed=flops // 256, transcendentals=0
        ),
    )(idx, *operands)


def finish_kernel(owned, at_ref, tables_ref, seat_ref, left_ref, right_ref, est_ref, fit_ref):
    members = tables_ref.shape[1]
    row = jnp.sum(tables_ref[...], axis=0, keepdims=True)
    shape = (members, members)
    same = lax.broadcasted_iota(jnp.int32, shape, 0) == lax.broadcasted_iota(jnp.int32, shape, 1)
    column = jnp.sum(
        jnp.where(same, jnp.broadcast_to(row, shape), 0.0), axis=1, keepdims=True
    )
    fit_ref[...] = jnp.sum(seat_ref[...] * column, axis=0, keepdims=True)[:, :owned]
    average = jnp.sum(row) / members
    variance = jnp.sum(jnp.square(row - average)) / members
    spread = jnp.sqrt(jnp.full((members, 1), variance + epsilon, jnp.float32))
    weights = (column - average) / spread / math.sqrt(members)
    scaled = left_ref[...].astype(jnp.float32) * weights
    high = scaled.astype(jnp.bfloat16)
    rest = scaled - high.astype(jnp.float32)
    middle = rest.astype(jnp.bfloat16)
    low = (rest - middle.astype(jnp.float32)).astype(jnp.bfloat16)
    total = None
    for term in (low, middle, high):
        part = lax.dot_general(
            term, right_ref[...], (((0,), (0,)), ((), ())), preferred_element_type=jnp.float32
        )
        total = part if total is None else total + part
    est_ref[...] = total


def finish(at, tables, seat, factor_left, factor_right, owned, row_share):
    devices, members = tables.shape
    columns = factor_right.shape[1]
    return pl.pallas_call(
        functools.partial(finish_kernel, owned),
        grid_spec=pltpu.PrefetchScalarGridSpec(
            num_scalar_prefetch=1,
            grid=(1,),
            in_specs=[
                pl.BlockSpec((devices, members), lambda n, at: (0, 0)),
                pl.BlockSpec((members, LANES), lambda n, at: (0, 0)),
                pl.BlockSpec((members, row_share), lambda n, at: (0, at[0])),
                pl.BlockSpec((members, columns), lambda n, at: (0, 0)),
            ],
            out_specs=[
                pl.BlockSpec((row_share, columns), lambda n, at: (0, 0)),
                pl.BlockSpec((1, owned), lambda n, at: (0, 0)),
            ],
        ),
        out_shape=[
            jax.ShapeDtypeStruct((row_share, columns), jnp.float32),
            jax.ShapeDtypeStruct((1, owned), jnp.float32),
        ],
        compiler_params=pltpu.CompilerParams(vmem_limit_bytes=VMEM_LIMITS[2]),
    )(at, tables, seat, factor_left, factor_right)


def sources(x_first):
    here = lax.axis_index("mp")
    x, y = here // SIDE, here % SIDE
    steps = jnp.array(STEPS, dtype=jnp.int32)
    if x_first:
        index = ((x - steps[None, :]) % SIDE) * SIDE + (y - steps[:, None]) % SIDE
    else:
        index = ((x - steps[:, None]) % SIDE) * SIDE + (y - steps[None, :]) % SIDE
    return index.reshape(-1).astype(jnp.int32)


def per_device(weight, layer_input, cotangent, factor_left, factor_right, seeds):
    members = factor_left.shape[0]
    owned = seeds.shape[0]
    rows = layer_input.shape[0]
    half = rows // 2
    quarter = rows // 4

    pieces = {True: layer_input[:half], False: layer_input[half:]}
    blocks = {}
    for o in (True, False):
        back, ahead, far0, far1 = first_ring(pieces[o], o)
        blocks[o] = [
            jnp.concatenate([pieces[o][s], back[s], ahead[s], far], axis=1)
            for s, far in ((slice(0, quarter), far0), (slice(quarter, half), far1))
        ]

    slots = jnp.pad(seeds, (0, LANES - owned), constant_values=-1)
    seat = slots[None, :] == jnp.arange(members, dtype=jnp.int32)[:, None]
    picked = seat.astype(jnp.bfloat16)
    contract = (((0,), (0,)), ((), ()))
    left_own = lax.dot_general(
        factor_left, picked, contract, preferred_element_type=jnp.float32
    ).astype(jnp.bfloat16)
    right_own = lax.dot_general(
        picked[:, :owned], factor_right, contract, preferred_element_type=jnp.float32
    )

    both = (True, False)
    ways = (1, -1)
    idx = jnp.concatenate([sources(o) for o in both])

    def send(arrays, o, sense):
        return [
            shift(a, 0, sense * way) if o else shift(a, sense * way, 0)
            for a, way in zip(arrays, ways)
        ]

    def terms(*given):
        out = []
        for base, o in ((0, True), (SIDE * SIDE, False)):
            for h in range(2):
                out.append([(arrays[o][h], base + SIDE * groups[h]) for arrays, groups in given])
        return out

    near = {o: send(blocks[o], o, 1) for o in both}
    far = {o: send(near[o], o, 1) for o in both}
    sums = stage(terms((near, (1, 2))), idx, weight, left_own, VMEM_LIMITS[0])
    far, sums, blocks = lax.optimization_barrier((far, sums, blocks))
    other = {o: send(blocks[o], o, -1) for o in both}
    sums = stage(terms((blocks, (0, 0)), (far, (3, 3))), idx, weight, left_own, VMEM_LIMITS[1], sums)
    everywhere = ("pop", "mp")
    devices = lax.axis_size("pop") * lax.axis_size("mp")
    seated = (seeds[:, None] == jnp.arange(members, dtype=jnp.int32)[None, :]).astype(jnp.float32)
    copies = stage(
        terms((other, (2, 1))), idx, weight, left_own, VMEM_LIMITS[2], sums,
        (right_own, cotangent, seated, devices),
    )
    tables = lax.all_to_all(copies, everywhere, 0, 0, tiled=True).reshape(devices, members)
    row_share = weight.shape[0] // lax.axis_size("pop")
    at = lax.axis_index("pop").astype(jnp.int32).reshape(1)
    estimate, fitness = finish(
        at, tables, seat.astype(jnp.float32), factor_left, factor_right, owned, row_share
    )
    return (estimate, fitness.reshape(owned))


def solution(mesh):
    placed = (P(None, "mp"), P("pop", "mp"), P("pop", "mp"), P(), P(None, "mp"), P("pop"))
    return jax.shard_map(
        per_device,
        mesh=mesh,
        in_specs=placed,
        out_specs=(P("pop", "mp"), P("pop")),
        check_vma=False,
    )
```

```python
import functools
import math

import jax
import jax.numpy as jnp
from jax import lax
from jax.experimental import pallas as pl
from jax.experimental.pallas import tpu as pltpu
from jax.sharding import PartitionSpec as P

D = 4096
FF = 16384
TOK = 128
SIDE = 4
STEPS = (0, 1, -1, 2)

perturb_scale = 0.25
epsilon = 1e-05

COLS = 256
LANES = 128
VMEM_LIMITS = (52 << 20, 24 << 20, 24 << 20)


def shift(piece, dx, dy):
    perm = [
        (x * SIDE + y, ((x + dx) % SIDE) * SIDE + (y + dy) % SIDE)
        for x in range(SIDE)
        for y in range(SIDE)
    ]
    return lax.ppermute(piece, "mp", perm)


def first_ring(piece, along_x):
    step = (lambda a, k: shift(a, k, 0)) if along_x else (lambda a, k: shift(a, 0, k))
    half = piece.shape[0] // 2
    back, ahead = step(piece, 1), step(piece, -1)
    return back, ahead, step(back[:half], 1), step(ahead[half:], -1)


def stage_kernel(terms, started, final, idx_ref, *refs):
    refs = list(refs)
    xs = [[refs.pop(0) for _ in block] for block in terms]
    w_ref, left_ref = refs.pop(0), refs.pop(0)
    sum_ref, sum_proj_ref = (refs.pop(0), refs.pop(0)) if started else (None, None)
    right_ref, cot_ref, seat_ref = [refs.pop(0) for _ in range(3)] if final else [None] * 3
    if final:
        table_ref, proj_ref, out_ref = refs
    else:
        out_ref, proj_ref = refs
    rows, extent = xs[0][0].shape
    width = extent // SIDE
    members = rows // TOK

    def product(b, ref):
        total = None
        for x_ref, place in zip(xs[b], terms[b]):
            parts = [
                ref[pl.ds(pl.multiple_of(idx_ref[place + k] * width, width), width), :]
                for k in range(SIDE)
            ]
            part = jnp.dot(
                x_ref[...], jnp.concatenate(parts, axis=0), preferred_element_type=jnp.float32
            )
            total = part if total is None else total + part
        return total

    @pl.when(pl.program_id(0) == 0)
    def _():
        for b in range(len(terms)):
            total = product(b, left_ref)
            if started:
                total += sum_proj_ref[b * rows : (b + 1) * rows, :]
            if not final:
                proj_ref[b * rows : (b + 1) * rows, :] = total
                continue
            for m in range(members):
                slot = b * members + m
                one = total[m * TOK : (m + 1) * TOK, slot : slot + 1]
                proj_ref[slot * TOK : (slot + 1) * TOK, :] = jnp.broadcast_to(
                    one * (perturb_scale / math.sqrt(D)), (TOK, LANES)
                )
        if final:
            out_ref[...] = jnp.zeros(out_ref.shape, jnp.float32)

    here = pl.ds(pl.multiple_of(pl.program_id(0) * COLS, COLS), COLS) if final else slice(None)
    ahead = product(0, w_ref)
    for b in range(len(terms)):
        base = ahead
        if b + 1 < len(terms):
            ahead = product(b + 1, w_ref)
        if started and not final:
            base += sum_ref[b * rows : (b + 1) * rows, here]
        if not final:
            out_ref[b * rows : (b + 1) * rows, :] = base
            continue
        for m in range(members):
            slot = b * members + m
            token = slice(m * TOK, (m + 1) * TOK)
            there = slice(slot * TOK, (slot + 1) * TOK)
            proj = proj_ref[there, :]
            right = right_ref[slot : slot + 1, here]
            cot = cot_ref[there, here].astype(jnp.float32)
            carried = sum_ref[there, here]
            sums = jnp.zeros((1, LANES), jnp.float32)
            for g in range(COLS // LANES):
                cols = slice(g * LANES, (g + 1) * LANES)
                rest = carried[:, cols] + proj * right[:, cols]
                act = jnp.maximum(base[token, cols] + rest, 0.0)
                term = cot[:, cols] * (act * act)
                sums += jnp.sum(term, axis=0, keepdims=True)
            out_ref[slot : slot + 1, :] += sums

    if final:

        @pl.when(pl.program_id(0) == pl.num_programs(0) - 1)
        def _():
            fitness = jnp.sum(out_ref[...], axis=1, keepdims=True) / -math.sqrt(TOK * FF)
            table = jnp.sum(seat_ref[...] * fitness, axis=0, keepdims=True)
            table_ref[...] = jnp.broadcast_to(table[None], table_ref.shape)


def stage(blocks, idx, weight, left_own, limit, sums=None, score=None):
    terms = tuple(tuple(place for _, place in block) for block in blocks)
    rows, extent = blocks[0][0][0].shape
    total = rows * len(blocks)
    depth, columns = weight.shape
    whole = lambda n, idx: (0, 0)
    tile = lambda n, idx: (0, n)
    once = pl.Buffered(1)
    operands = [piece for block in blocks for piece, _ in block]
    placed = pl.BlockSpec(memory_space=pltpu.VMEM)
    final = score is not None
    in_specs = [
        placed if final else pl.BlockSpec((rows, extent), whole, pipeline_mode=once)
    ] * len(operands)
    in_specs += [
        pl.BlockSpec((depth, COLS), tile),
        placed if final else pl.BlockSpec((depth, LANES), whole, pipeline_mode=once),
    ]
    operands += [weight, left_own]
    block = pl.BlockSpec((total, COLS), tile)
    if sums is not None:
        carried = [block, pl.BlockSpec((total, LANES), whole, pipeline_mode=once)]
        in_specs += [placed, placed] if final else carried
        operands += list(sums)
    if score is None:
        out_specs, scratch = [block, pl.BlockSpec((total, LANES), whole)], []
        out_shape = [
            jax.ShapeDtypeStruct((total, columns), jnp.float32),
            jax.ShapeDtypeStruct((total, LANES), jnp.float32),
        ]
    else:
        members = total // TOK
        in_specs += [placed] * 3
        operands += list(score[:3])
        devices, table = score[3], score[2].shape[1]
        out_specs = pl.BlockSpec((devices, 1, table), lambda n, idx: (0, 0, 0))
        out_shape = jax.ShapeDtypeStruct((devices, 1, table), jnp.float32)
        scratch = [
            pltpu.VMEM((total, LANES), jnp.float32),
            pltpu.VMEM((members, LANES), jnp.float32),
        ]
    flops = 2 * sum(len(t) for t in terms) * rows * extent * columns
    return pl.pallas_call(
        functools.partial(stage_kernel, terms, sums is not None, score is not None),
        grid_spec=pltpu.PrefetchScalarGridSpec(
            num_scalar_prefetch=1,
            grid=(columns // COLS,),
            in_specs=in_specs,
            out_specs=out_specs,
            scratch_shapes=scratch,
        ),
        out_shape=out_shape,
        compiler_params=pltpu.CompilerParams(vmem_limit_bytes=limit),
        cost_estimate=pl.CostEstimate(
            flops=flops, bytes_accessed=flops // 256, transcendentals=0
        ),
    )(idx, *operands)


def finish_kernel(owned, at_ref, tables_ref, seat_ref, left_ref, right_ref, est_ref, fit_ref):
    members = tables_ref.shape[1]
    row = jnp.sum(tables_ref[...], axis=0, keepdims=True)
    shape = (members, members)
    same = lax.broadcasted_iota(jnp.int32, shape, 0) == lax.broadcasted_iota(jnp.int32, shape, 1)
    column = jnp.sum(
        jnp.where(same, jnp.broadcast_to(row, shape), 0.0), axis=1, keepdims=True
    )
    fit_ref[...] = jnp.sum(seat_ref[...] * column, axis=0, keepdims=True)[:, :owned]
    average = jnp.sum(row) / members
    variance = jnp.sum(jnp.square(row - average)) / members
    spread = jnp.sqrt(jnp.full((members, 1), variance + epsilon, jnp.float32))
    weights = (column - average) / spread / math.sqrt(members)
    scaled = left_ref[...].astype(jnp.float32) * weights
    high = scaled.astype(jnp.bfloat16)
    rest = scaled - high.astype(jnp.float32)
    middle = rest.astype(jnp.bfloat16)
    low = (rest - middle.astype(jnp.float32)).astype(jnp.bfloat16)
    total = None
    for term in (low, middle, high):
        part = lax.dot_general(
            term, right_ref[...], (((0,), (0,)), ((), ())), preferred_element_type=jnp.float32
        )
        total = part if total is None else total + part
    est_ref[...] = total


def finish(at, tables, seat, factor_left, factor_right, owned, row_share):
    devices, members = tables.shape
    columns = factor_right.shape[1]
    return pl.pallas_call(
        functools.partial(finish_kernel, owned),
        grid_spec=pltpu.PrefetchScalarGridSpec(
            num_scalar_prefetch=1,
            grid=(1,),
            in_specs=[
                pl.BlockSpec((devices, members), lambda n, at: (0, 0)),
                pl.BlockSpec((members, LANES), lambda n, at: (0, 0)),
                pl.BlockSpec((members, row_share), lambda n, at: (0, at[0])),
                pl.BlockSpec((members, columns), lambda n, at: (0, 0)),
            ],
            out_specs=[
                pl.BlockSpec((row_share, columns), lambda n, at: (0, 0)),
                pl.BlockSpec((1, owned), lambda n, at: (0, 0)),
            ],
        ),
        out_shape=[
            jax.ShapeDtypeStruct((row_share, columns), jnp.float32),
            jax.ShapeDtypeStruct((1, owned), jnp.float32),
        ],
        compiler_params=pltpu.CompilerParams(vmem_limit_bytes=VMEM_LIMITS[2]),
    )(at, tables, seat, factor_left, factor_right)


def sources(x_first):
    here = lax.axis_index("mp")
    x, y = here // SIDE, here % SIDE
    steps = jnp.array(STEPS, dtype=jnp.int32)
    if x_first:
        index = ((x - steps[None, :]) % SIDE) * SIDE + (y - steps[:, None]) % SIDE
    else:
        index = ((x - steps[:, None]) % SIDE) * SIDE + (y - steps[None, :]) % SIDE
    return index.reshape(-1).astype(jnp.int32)


def per_device(weight, layer_input, cotangent, factor_left, factor_right, seeds):
    members = factor_left.shape[0]
    owned = seeds.shape[0]
    rows = layer_input.shape[0]
    half = rows // 2
    quarter = rows // 4

    pieces = {True: layer_input[:half], False: layer_input[half:]}
    blocks = {}
    for o in (True, False):
        back, ahead, far0, far1 = first_ring(pieces[o], o)
        blocks[o] = [
            jnp.concatenate([pieces[o][s], back[s], ahead[s], far], axis=1)
            for s, far in ((slice(0, quarter), far0), (slice(quarter, half), far1))
        ]

    slots = jnp.pad(seeds, (0, LANES - owned), constant_values=-1)
    seat = slots[None, :] == jnp.arange(members, dtype=jnp.int32)[:, None]
    picked = seat.astype(jnp.bfloat16)
    contract = (((0,), (0,)), ((), ()))
    left_own = lax.dot_general(
        factor_left, picked, contract, preferred_element_type=jnp.float32
    ).astype(jnp.bfloat16)
    right_own = lax.dot_general(
        picked[:, :owned], factor_right, contract, preferred_element_type=jnp.float32
    )

    both = (True, False)
    ways = (1, -1)
    idx = jnp.concatenate([sources(o) for o in both])

    def send(arrays, o, sense):
        return [
            shift(a, 0, sense * way) if o else shift(a, sense * way, 0)
            for a, way in zip(arrays, ways)
        ]

    def terms(*given):
        out = []
        for base, o in ((0, True), (SIDE * SIDE, False)):
            for h in range(2):
                out.append([(arrays[o][h], base + SIDE * groups[h]) for arrays, groups in given])
        return out

    near = {o: send(blocks[o], o, 1) for o in both}
    far = {o: send(near[o], o, 1) for o in both}
    sums = stage(terms((near, (1, 2))), idx, weight, left_own, VMEM_LIMITS[0])
    far, sums, blocks = lax.optimization_barrier((far, sums, blocks))
    other = {o: send(blocks[o], o, -1) for o in both}
    sums = stage(terms((blocks, (0, 0)), (far, (3, 3))), idx, weight, left_own, VMEM_LIMITS[1], sums)
    everywhere = ("pop", "mp")
    devices = lax.axis_size("pop") * lax.axis_size("mp")
    seated = (seeds[:, None] == jnp.arange(members, dtype=jnp.int32)[None, :]).astype(jnp.float32)
    copies = stage(
        terms((other, (2, 1))), idx, weight, left_own, VMEM_LIMITS[2], sums,
        (right_own, cotangent, seated, devices),
    )
    tables = lax.all_to_all(copies, everywhere, 0, 0, tiled=True).reshape(devices, members)
    row_share = weight.shape[0] // lax.axis_size("pop")
    at = lax.axis_index("pop").astype(jnp.int32).reshape(1)
    estimate, fitness = finish(
        at, tables, seat.astype(jnp.float32), factor_left, factor_right, owned, row_share
    )
    return (estimate, fitness.reshape(owned))


def solution(mesh):
    placed = (P(None, "mp"), P("pop", "mp"), P("pop", "mp"), P(), P(None, "mp"), P("pop"))
    return jax.shard_map(
        per_device,
        mesh=mesh,
        in_specs=placed,
        out_specs=(P("pop", "mp"), P("pop")),
        check_vma=False,
    )
```
